32 devices in a mesh: dp: 4 (over y, x), ctx: 2 (over core), head: 4 (over z).
Axes of the slice: x: 2, y: 2, z: 4, core: 2. Of those that a mesh axis runs over, the one named last changes fastest.
Arguments:
- inputs: bfloat16 [4, 256, 4096], P('dp', 'ctx', 'head'), may hold values from -6 to 6
- step_rate: float32 [4, 256, 4096], P('dp', 'ctx', 'head'), may hold values from 0 to 12
- key_rows: bfloat16 [4, 256, 16], P('dp', 'ctx'), may hold values from -5 to 5
- query_rows: bfloat16 [4, 256, 16], P('dp', 'ctx'), may hold values from -1.5 to 1.5
- grad_out: bfloat16 [4, 256, 4096], P('dp', 'ctx', 'head'), may hold values from -6 to 6
Outputs:
- grad_inputs: bfloat16 [4, 256, 4096], P('dp', ('ctx', 'head'))
- grad_rate: bfloat16 [4, 256, 4096], P('dp', ('ctx', 'head'))
- grad_keys: float32 [4, 256, 16], P('dp', ('ctx', 'head'))
- grad_queries: float32 [4, 256, 16], P('dp', ('ctx', 'head'))
The draws below stay inside these ranges and needn't reach their ends.
All inputs are finite; a program needn't handle non-finite values.
Results may differ from the reference program's by a relative error of at most 0.0018.
Values may be sent and summed in bfloat16 or wider, within the bound.
No kernel may reach another device: no remote copies, remote signals or barrier semaphores. Data moves between devices by JAX's collectives and lax.ppermute only.
A program may use at most 64 MiB of HBM per device.

```python
import math
import jax
import jax.numpy as jnp
from jax import lax

INNER = 4096
STATE = 16
BLOCK = 16
SEQUENCE_COUNT = 4
SEQUENCE_LENGTH = 256


def draw_step_rate(key, part):
    key = jax.random.fold_in(key, 7)
    every_key = jax.random.split(key, 7)
    shape_ch = (SEQUENCE_COUNT, 1, INNER)
    rate_logarithm = jax.random.uniform(every_key[0], shape_ch, jnp.float32, math.log(3e-05), math.log(0.08))
    positions = jnp.arange(SEQUENCE_LENGTH, dtype=jnp.float32)[None, :, None]
    phase = jax.random.uniform(every_key[3], (SEQUENCE_COUNT, 1, 1), jnp.float32, 0.0, 2.0 * math.pi)
    steady_input = jnp.exp(0.7 * jnp.sin(6.0 * math.pi * positions / SEQUENCE_LENGTH + phase))
    noisy_input = jnp.exp(jax.random.uniform(every_key[4], (SEQUENCE_COUNT, SEQUENCE_LENGTH, INNER), jnp.float32, -0.7, 0.7))
    spike_mask = jax.random.bernoulli(every_key[5], 8.0 / SEQUENCE_LENGTH, (SEQUENCE_COUNT, SEQUENCE_LENGTH, 1))
    spike_value = jax.random.uniform(every_key[6], (SEQUENCE_COUNT, SEQUENCE_LENGTH, 1), jnp.float32, 4.0, 12.0)
    rate_values = jnp.where(spike_mask, spike_value, jnp.exp(rate_logarithm) * steady_input * noisy_input)
    return rate_values.astype(jnp.float32)


def block_levels(stream_key, extent, pieces, least, top_value):
    def one(dim, shards_of):
        draws = jax.random.uniform(jax.random.fold_in(jax.random.fold_in(stream_key, 6), dim), (shards_of,), jnp.float32, least / len(pieces), top_value / len(pieces))
        return jnp.repeat(jnp.exp(draws), extent[dim] // shards_of).reshape((-1,) + (1,) * (len(extent) - dim - 1))

    level = one(*pieces[0])
    for cut in pieces[1:]:
        level = level * one(*cut)
    return level


def normal_values(key, extent, width, limit, cuts=(), held_as=jnp.bfloat16):
    drawn = width * jax.random.normal(key, extent, jnp.float32)
    if cuts:
        drawn = drawn * block_levels(key, extent, cuts, -0.22, 0.18)
    return jnp.clip(drawn, -limit, limit).astype(held_as)


def setup_inputs(seed: int = 0) -> dict:
    arg_keys = jax.random.split(jax.random.key(seed), 6)
    return {
        "inputs": normal_values(arg_keys[0], (SEQUENCE_COUNT, SEQUENCE_LENGTH, INNER), 1.0, 6.0, ((0, 4), (1, 2), (2, 4))),
        "step_rate": draw_step_rate(jax.random.fold_in(arg_keys[5], 71), 0),
        "key_rows": normal_values(arg_keys[2], (SEQUENCE_COUNT, SEQUENCE_LENGTH, STATE), 1.0, 5.0, ((0, 4), (1, 2))),
        "query_rows": normal_values(arg_keys[3], (SEQUENCE_COUNT, SEQUENCE_LENGTH, STATE), STATE ** -0.5, 1.5, ((0, 4), (1, 2))),
        "grad_out": normal_values(arg_keys[4], (SEQUENCE_COUNT, SEQUENCE_LENGTH, INNER), 1.0, 6.0, ((0, 4), (1, 2), (2, 4))),
    }


def affine(earlier, subsequent):
    return (earlier[0] * subsequent[0], subsequent[0] * earlier[1] + subsequent[1])


def block_setup(inputs, rate_values, key_blk):
    keys_sq = key_blk * key_blk
    key_norm = jnp.sum(keys_sq, axis=1)
    denominator = 1.0 + rate_values * key_norm[:, None]
    step_size = rate_values / denominator
    decays = 1.0 - step_size[:, None, :] * keys_sq[:, :, None]
    drives = (step_size * inputs)[:, None, :] * key_blk[:, :, None]
    return keys_sq, denominator, step_size, decays, drives


def reverse_states(decays, emitted, carried):
    following = jnp.concatenate([decays[1:], jnp.ones_like(decays[:1])], axis=0)
    products, accumulated = lax.associative_scan(affine, (following[::-1], emitted[::-1]), axis=0)
    return (accumulated + products * carried[None])[::-1]


def block_grads(inputs, rate_values, key_blk, query_blk, grad_blk, start_state, carried):
    keys_sq, denominator, step_size, decays, drives = block_setup(inputs, rate_values, key_blk)
    products, accumulated = lax.associative_scan(affine, (decays, drives), axis=0)
    states = accumulated + products * start_state[None]
    previous = jnp.concatenate([start_state[None], states[:-1]], axis=0)
    emitted = grad_blk[:, None, :] * query_blk[:, :, None]
    state_grads = reverse_states(decays, emitted, carried)
    key_dot = jnp.sum(state_grads * key_blk[:, :, None], axis=1)
    weighted = state_grads * previous
    weighted_sum = jnp.sum(weighted * keys_sq[:, :, None], axis=1)
    grad_in = step_size * key_dot
    grad_step = inputs * key_dot - weighted_sum
    grad_rate = grad_step / (denominator * denominator)
    term_drive = jnp.sum(state_grads * (step_size * inputs)[:, None, :], axis=2)
    term_decay = jnp.sum(weighted * step_size[:, None, :], axis=2)
    term_norm = jnp.sum(grad_step * step_size * step_size, axis=1)
    grad_key = term_drive - 2.0 * key_blk * (term_decay + term_norm[:, None])
    grad_query = jnp.sum(grad_blk[:, None, :] * states, axis=2)
    return decays[0] * state_grads[0], (grad_in, grad_rate, grad_key, grad_query)


def one_sequence(sequence):
    inputs, step_rate, key_rows, query_rows, grad_out = sequence
    num_blocks = inputs.shape[0] // BLOCK
    channels = inputs.shape[1]
    state_dim = key_rows.shape[1]

    def to_blocks(array_in):
        return array_in.astype(jnp.float32).reshape(num_blocks, BLOCK, array_in.shape[1])

    blocked = (to_blocks(inputs), to_blocks(step_rate), to_blocks(key_rows), to_blocks(query_rows), to_blocks(grad_out))

    def forward(carried, block_in):
        _, _, _, decays, drives = block_setup(block_in[0], block_in[1], block_in[2])
        products, accumulated = lax.associative_scan(affine, (decays, drives), axis=0)
        return accumulated[-1] + products[-1] * carried, carried

    zero_state = jnp.zeros((state_dim, channels), jnp.float32)
    _, block_starts = lax.scan(forward, zero_state, blocked[:3])

    def backward(carried, block_in):
        return block_grads(block_in[0], block_in[1], block_in[2], block_in[3], block_in[4], block_in[5], carried)

    _, results = lax.scan(backward, zero_state, blocked + (block_starts,), reverse=True)
    grad_in, grad_rate, grad_key, grad_query = results
    return (grad_in.reshape(-1, channels).astype(jnp.bfloat16),
            grad_rate.reshape(-1, channels).astype(jnp.bfloat16),
            grad_key.reshape(-1, state_dim),
            grad_query.reshape(-1, state_dim))


def reference(inputs, step_rate, key_rows, query_rows, grad_out):
    return lax.map(one_sequence, (inputs, step_rate, key_rows, query_rows, grad_out))
```

```python
import functools

import jax
import jax.numpy as jnp
from jax import lax
from jax.experimental import pallas as pl
from jax.experimental.pallas import tpu as pltpu
from jax.sharding import PartitionSpec as P

BLOCK = 16
LANES = 128
SUB = 8
UNROLL = 8
CHUNKS = 1
VMEM_LIMIT = 20 * 1024 * 1024


def affine(earlier, subsequent):
    return (earlier[0] * subsequent[0], subsequent[0] * earlier[1] + subsequent[1])


def prefix(array, axis, identity, reverse):
    size, position = (lax.axis_size(axis), lax.axis_index(axis))
    everything = jax.tree.map(lambda part: lax.all_gather(part, axis), array)
    start = jax.tree.map(
        lambda part, zero: jnp.broadcast_to(jnp.asarray(zero, part.dtype), part.shape),
        array,
        identity,
    )

    def hop(k, before):
        at = size - 1 - k if reverse else k
        reached = at > position if reverse else at < position
        new = affine(before, jax.tree.map(lambda part: part[at], everything))
        return jax.tree.map(lambda a, b: jnp.where(reached, a, b), new, before)

    return lax.fori_loop(0, size, hop, start)


def group_summary(inputs, step_rate, key_rows, query_rows, grad_out):
    tokens, channels = inputs.shape[1:]
    state_dim = key_rows.shape[2]
    num_blocks = tokens // BLOCK

    def to_blocks(array_in):
        return array_in[0].astype(jnp.float32).reshape(num_blocks, BLOCK, array_in.shape[2])

    def summarize(carried, block_in):
        x, rate, key_blk, query_blk, grad_blk = block_in
        keys_sq = key_blk * key_blk
        step = rate / (1.0 + rate * jnp.sum(keys_sq, axis=1)[:, None])
        decays = 1.0 - step[:, None, :] * keys_sq[:, :, None]
        drives = (step * x)[:, None, :] * key_blk[:, :, None]
        before = jnp.cumprod(decays, axis=0)
        suffix = jnp.cumprod(decays[::-1], axis=0)[::-1]
        after = jnp.concatenate([suffix[1:], jnp.ones_like(decays[:1])], axis=0)
        total = before[-1]
        end = jnp.sum(drives * after, axis=0)
        back = jnp.sum(grad_blk[:, None, :] * query_blk[:, :, None] * before, axis=0)
        return (
            carried[0] * total,
            total * carried[1] + end,
            carried[2] + carried[0] * back,
        ), None

    zero = jnp.zeros((state_dim, channels), jnp.float32)
    blocked = tuple(map(to_blocks, (inputs, step_rate, key_rows, query_rows, grad_out)))
    return lax.scan(summarize, (jnp.ones_like(zero), zero, zero), blocked)[0]


def columns(matrix, base):
    rows, tokens = matrix.shape
    turned = pltpu.roll(matrix, lax.rem(tokens - base, tokens), 1)
    return [jnp.broadcast_to(turned[:, u : u + 1], (rows, LANES)) for u in range(UNROLL)]


def halves(value):
    return [value[at : at + SUB] for at in range(0, value.shape[0], SUB)]


def row(ref, tile, t):
    return ref[tile, pl.ds(t, SUB, stride=0), :]


def tile_at(j):
    return pl.ds(j * LANES, LANES)


def lane_sums(values):
    ones = jnp.ones((SUB, LANES), jnp.bfloat16)

    def product(part):
        return lax.dot_general(
            ones, part, (((1,), (1,)), ((), ())), preferred_element_type=jnp.float32
        )

    high = values.astype(jnp.bfloat16)
    low = (values - high.astype(jnp.float32)).astype(jnp.bfloat16)
    return product(high) + product(low)


def first_kernel(backwards, has_entry, *refs):
    x_ref, rate_ref, key_ref, query_ref, go_ref = refs[:5]
    entry_ref = refs[5] if has_entry else None
    path_ref, end_ref, rows_ref, step_ref, drive_ref, x32_ref, go32_ref, inverse_ref = refs[
        5 + has_entry :
    ]
    states, tokens = key_ref.shape[1:]
    tiles = x_ref.shape[2] // LANES
    key = key_ref[0].astype(jnp.float32)
    query = query_ref[0].astype(jnp.float32)
    rows_ref[0] = key
    rows_ref[1] = query
    key_norm = jnp.sum(key * key, axis=0, keepdims=True)
    norm = jnp.transpose(jnp.broadcast_to(key_norm, (LANES, tokens)))
    for j in range(tiles):
        rate = rate_ref[0, :, tile_at(j)]
        x = x_ref[0, :, tile_at(j)].astype(jnp.float32)
        inverse = 1.0 / (1.0 + rate * norm)
        step = rate * inverse
        inverse_ref[j, :tokens] = inverse
        step_ref[j, :tokens] = step
        x32_ref[j, :tokens] = x
        drive_ref[j, :tokens] = step * x
        go32_ref[j, :tokens] = go_ref[0, :, tile_at(j)].astype(jnp.float32)

    if has_entry:
        entry = [halves(entry_ref[:, tile_at(j)]) for j in range(tiles)]
    else:
        entry = [[jnp.zeros((SUB, LANES), jnp.float32)] * (states // SUB)] * tiles

    def finish(state):
        for j in range(tiles):
            end_ref[:, tile_at(j)] = jnp.concatenate(state[j], axis=0)

    def run_states():
        def block(b, state):
            base = b * UNROLL
            keys = columns(key, base)
            state = [list(part) for part in state]
            for u in range(UNROLL):
                k = halves(keys[u])
                k2 = [part * part for part in k]
                for j in range(tiles):
                    step = row(step_ref, j, base + u)
                    drive = row(drive_ref, j, base + u)
                    for h in range(len(k)):
                        state[j][h] = (1.0 - step * k2[h]) * state[j][h] + drive * k[h]
                        path_ref[base + u, pl.ds(h * SUB, SUB), tile_at(j)] = state[j][h]
            return state

        finish(lax.fori_loop(0, tokens // UNROLL, block, entry))

    def run_grads():
        def block(i, state):
            base = tokens - UNROLL - i * UNROLL
            keys = columns(key, base)
            queries = columns(query, base)
            state = [list(part) for part in state]
            for u in reversed(range(UNROLL)):
                k2 = [part * part for part in halves(keys[u])]
                q = halves(queries[u])
                for j in range(tiles):
                    step = row(step_ref, j, base + u)
                    go = row(go32_ref, j, base + u)
                    for h in range(len(q)):
                        grad = go * q[h] + state[j][h]
                        path_ref[base + u, pl.ds(h * SUB, SUB), tile_at(j)] = grad
                        state[j][h] = (1.0 - step * k2[h]) * grad
            return state

        finish(lax.fori_loop(0, tokens // UNROLL, block, entry))

    choose(backwards, run_grads, run_states)


def choose(flag, if_set, if_not):
    if flag is None:
        group = lax.axis_index("ctx")
        pl.when(group != 0)(if_set)
        pl.when(group == 0)(if_not)
    else:
        (if_set if flag else if_not)()


def second_kernel(onwards_here, last, heads, has_start, has_before, *refs):
    refs = list(refs)
    entry_ref, path_ref, rows_ref, step_ref, drive_ref, x32_ref, go32_ref, inverse_ref = refs[:8]
    del refs[:8]
    start_ref = refs.pop(0) if has_start else None
    before_ref = refs.pop(0) if has_before else None
    message_ref, sums_ref, dot_ref, weighted_ref, key_part_ref, query_part_ref, norm_ref = refs
    states, tokens = rows_ref.shape[1:]
    tiles = step_ref.shape[0]
    width = tiles * LANES
    key = rows_ref[0]
    query = rows_ref[1]
    pair = range(states // SUB)

    def path_at(t, h, j):
        return path_ref[t, pl.ds(h * SUB, SUB), tile_at(j)]

    def step_through(back, advance):
        def block(i, state):
            base = tokens - UNROLL - i * UNROLL if back else i * UNROLL
            keys = columns(key, base)
            queries = columns(query, base)
            state = [list(part) for part in state]
            for u in reversed(range(UNROLL)) if back else range(UNROLL):
                t = base + u
                k, q = halves(keys[u]), halves(queries[u])
                k2 = [part * part for part in k]
                sums = None
                for j in range(tiles):
                    step, drive, go = (
                        row(ref, j, t) for ref in (step_ref, drive_ref, go32_ref)
                    )
                    dots, weights, terms = [], [], []
                    for h in pair:
                        decay = 1.0 - step * k2[h]
                        grad, here, previous, state[j][h] = advance(
                            t, u, h, j, state[j][h], decay, drive, go, k[h], q[h]
                        )
                        weight = grad * previous
                        dots.append(grad * k[h])
                        weights.append(weight * k2[h])
                        terms += [grad * drive, weight * step, here * go]
                    dot_ref[j, pl.ds(pl.multiple_of(t * SUB, SUB), SUB), :] = sum(dots[1:], dots[0])
                    weighted_ref[j, pl.ds(pl.multiple_of(t * SUB, SUB), SUB), :] = sum(
                        weights[1:], weights[0]
                    )
                    sums = terms if j == 0 else [a + b for a, b in zip(sums, terms)]
                for h in pair:
                    by_drive, by_decay, by_query = sums[3 * h : 3 * h + 3]
                    at = pl.ds(pl.multiple_of(t * states + h * SUB, SUB), SUB)
                    key_part_ref[at, :] = by_drive - (2.0 * k[h]) * by_decay
                    query_part_ref[at, :] = by_query
            return state

        entry = [halves(entry_ref[:, tile_at(j)]) for j in range(tiles)]
        lax.fori_loop(0, tokens // UNROLL, block, entry)

    def backwards(t, u, h, j, state, decay, drive, go, k, q):
        grad = go * q + state
        earlier = path_at(jnp.maximum(t - 1, 0), h, j)
        if u == 0:
            start = start_ref[pl.ds(h * SUB, SUB), tile_at(j)] if has_start else 0.0
            earlier = jnp.where(t == 0, start, earlier)
        return grad, path_at(t, h, j), earlier, decay * grad

    def onwards(t, u, h, j, state, decay, drive, go, k, q):
        here = decay * state + drive * k
        return path_at(t, h, j), here, state, here

    choose(onwards_here, lambda: step_through(False, onwards), lambda: step_through(True, backwards))

    part = tokens // heads
    rows = 2 * SUB

    def finish(i, _):
        base = pl.multiple_of(i * rows, rows)
        to = pl.ds(pl.multiple_of(lax.rem(base, part), rows), rows)
        head = lax.div(base, part)
        norm_sum = None
        for j in range(tiles):
            dot, weighted = (
                sum(ref[j, pl.ds(base * SUB + s, rows, stride=SUB), :] for s in range(SUB))
                for ref in (dot_ref, weighted_ref)
            )
            step, x, inverse = (
                ref[j, pl.ds(base, rows), :] for ref in (step_ref, x32_ref, inverse_ref)
            )
            grad_step = x * dot - weighted
            message_ref[head, to, tile_at(j)] = (step * dot).astype(jnp.bfloat16)
            message_ref[head, to, tile_at(tiles + j)] = (grad_step * inverse * inverse).astype(
                jnp.bfloat16
            )
            term = grad_step * step * step
            norm_sum = term if j == 0 else norm_sum + term
        norm_ref[pl.ds(base, rows), :] = norm_sum
        return _

    lax.fori_loop(0, tokens // rows, finish, 0)
    norm_row = lane_sums(norm_ref[...])[:1]
    for n in range(states):
        at = pl.ds(n, tokens, stride=states)
        sums_ref[n : n + 1, :] = lane_sums(key_part_ref[at, :])[:1]
        sums_ref[states + n : states + n + 1, :] = lane_sums(query_part_ref[at, :])[:1]
    sums_ref[:states] = sums_ref[:states] - 2.0 * key * norm_row
    if has_before:
        sums_ref[...] = sums_ref[...] + before_ref[...]
    if last:
        quarters = 2 * states // SUB
        lane = lax.broadcasted_iota(jnp.int32, (SUB, tokens), 1) // part
        for h in range(heads):
            packed = None
            for i in range(quarters):
                turned = pltpu.roll(sums_ref[SUB * i : SUB * i + SUB], ((i - h) * part) % tokens, 1)
                packed = turned if packed is None else jnp.where(lane == i, turned, packed)
            high = packed.astype(jnp.bfloat16).astype(jnp.float32)
            both = jnp.concatenate([high, packed - high], axis=0).astype(jnp.bfloat16)
            message_ref[h, :rows, pl.ds(2 * width, LANES)] = both
            message_ref[h, rows:, pl.ds(2 * width, LANES)] = jnp.zeros(
                (part - rows, LANES), jnp.bfloat16
            )


def gather_kernel(heads, chunks, *refs):
    messages, (in_ref, rate_ref, key_ref, query_ref) = refs[:chunks], refs[chunks:]
    states, part = key_ref.shape[1:]
    channels = in_ref.shape[2] // heads
    width = channels // chunks
    total = None
    for s in range(heads):
        for c, message in enumerate(messages):
            to = pl.ds(s * channels + c * width, width)
            in_ref[0, :, to] = message[s, :, pl.ds(0, width)]
            rate_ref[0, :, to] = message[s, :, pl.ds(width, width)]
        both = messages[-1][s, :16, pl.ds(2 * width, LANES)].astype(jnp.float32)
        both = both[:8] + both[8:]
        total = both if total is None else total + both
    for i in range(states // 8):
        key_ref[0, 8 * i : 8 * i + 8] = total[:, i * part : (i + 1) * part]
        at = states // 8 + i
        query_ref[0, 8 * i : 8 * i + 8] = total[:, at * part : (at + 1) * part]


def shards(inputs, step_rate, key_rows, query_rows, grad_out):
    _, tokens, channels = inputs.shape
    states = key_rows.shape[2]
    heads = lax.axis_size("head")
    groups = lax.axis_size("ctx")
    width = channels // CHUNKS
    part = tokens // heads
    key_cols = jnp.swapaxes(key_rows, 1, 2)
    query_cols = jnp.swapaxes(query_rows, 1, 2)
    f32 = jnp.float32
    params = pltpu.CompilerParams(vmem_limit_bytes=VMEM_LIMIT)
    whole = pl.BlockSpec(memory_space=pltpu.VMEM)
    plane = pltpu.VMEM((width // LANES, tokens + SUB, LANES), f32)

    def first(c, backwards, entry=None):
        wide = pl.BlockSpec((1, tokens, width), lambda i: (0, 0, c))
        specs = [wide, wide, whole, whole, wide]
        arrays = [inputs, step_rate, key_cols, query_cols, grad_out]
        if entry is not None:
            specs, arrays = specs + [whole], arrays + [entry]
        return pl.pallas_call(
            functools.partial(first_kernel, backwards, entry is not None),
            grid=(1,),
            in_specs=specs,
            out_specs=[whole] * 8,
            out_shape=[
                pltpu.VMEM((tokens, states, width), f32),
                jax.ShapeDtypeStruct((states, width), f32),
                pltpu.VMEM((2, states, tokens), f32),
            ]
            + [plane] * 5,
            compiler_params=params,
        )(*arrays)

    def second(c, onwards_here, entry, carried, start, before):
        last = c == CHUNKS - 1
        wide_message = 2 * width + (LANES if last else 0)
        extra = [a for a in (start, before) if a is not None]
        parts = pltpu.VMEM((width // LANES, (tokens + 1) * SUB, LANES), f32)
        sums = pltpu.VMEM(((tokens + 1) * states, LANES), f32)
        return pl.pallas_call(
            functools.partial(
                second_kernel, onwards_here, last, heads, start is not None, before is not None
            ),
            in_specs=[whole] * (8 + len(extra)),
            out_specs=[whole, whole],
            out_shape=[
                jax.ShapeDtypeStruct((heads, part, wide_message), jnp.bfloat16),
                pltpu.VMEM((2 * states, tokens), f32),
            ],
            scratch_shapes=[parts, parts, sums, sums, pltpu.VMEM((tokens, LANES), f32)],
            compiler_params=params,
        )(entry, *carried, *extra)

    work = []
    if groups == 2:
        here = None
        for c in range(CHUNKS):
            path, end, *carried = first(c, here)
            entry = lax.ppermute(end, "ctx", [(0, 1), (1, 0)])
            work.append((entry, [path] + carried, None))
    else:
        here = False
        product, end, back = group_summary(inputs, step_rate, key_rows, query_rows, grad_out)
        unit = (jnp.ones_like(product), jnp.zeros_like(product))
        starts = prefix((product, end), "ctx", unit, False)[1]
        entries = prefix((product, back), "ctx", unit, True)[1]
        for c in range(CHUNKS):
            at = slice(c * width, (c + 1) * width)
            path, _, *carried = first(c, here, starts[:, at])
            work.append((entries[:, at], [path] + carried, starts[:, at]))

    sums = None
    arrived = []
    for c, (entry, carried, start) in enumerate(work):
        message, sums = second(c, here, entry, carried, start, sums)
        arrived.append(lax.all_to_all(message, "head", split_axis=0, concat_axis=0, tiled=True))

    grad_in, grad_rate, grad_key, grad_query = pl.pallas_call(
        functools.partial(gather_kernel, heads, CHUNKS),
        in_specs=[whole] * CHUNKS,
        out_specs=[whole] * 4,
        out_shape=[
            jax.ShapeDtypeStruct((1, part, heads * channels), jnp.bfloat16),
            jax.ShapeDtypeStruct((1, part, heads * channels), jnp.bfloat16),
            jax.ShapeDtypeStruct((1, states, part), f32),
            jax.ShapeDtypeStruct((1, states, part), f32),
        ],
        compiler_params=params,
    )(*arrived)
    return (grad_in, grad_rate, jnp.swapaxes(grad_key, 1, 2), jnp.swapaxes(grad_query, 1, 2))


def solution(mesh):
    placed = (
        P("dp", "ctx", "head"),
        P("dp", "ctx", "head"),
        P("dp", "ctx", None),
        P("dp", "ctx", None),
        P("dp", "ctx", "head"),
    )
    spread = P("dp", ("ctx", "head"), None)
    return jax.shard_map(
        shards, mesh=mesh, in_specs=placed, out_specs=(spread,) * 4, check_vma=False
    )
```

```python
import functools

import jax
import jax.numpy as jnp
from jax import lax
from jax.experimental import pallas as pl
from jax.experimental.pallas import tpu as pltpu
from jax.sharding import PartitionSpec as P

BLOCK = 16
LANES = 128
SUB = 8
UNROLL = 8
CHUNKS = 2
VMEM_LIMIT = 20 * 1024 * 1024


def affine(earlier, subsequent):
    return (earlier[0] * subsequent[0], subsequent[0] * earlier[1] + subsequent[1])


def prefix(array, axis, identity, reverse):
    size, position = (lax.axis_size(axis), lax.axis_index(axis))
    everything = jax.tree.map(lambda part: lax.all_gather(part, axis), array)
    start = jax.tree.map(
        lambda part, zero: jnp.broadcast_to(jnp.asarray(zero, part.dtype), part.shape),
        array,
        identity,
    )

    def hop(k, before):
        at = size - 1 - k if reverse else k
        reached = at > position if reverse else at < position
        new = affine(before, jax.tree.map(lambda part: part[at], everything))
        return jax.tree.map(lambda a, b: jnp.where(reached, a, b), new, before)

    return lax.fori_loop(0, size, hop, start)


def group_summary(inputs, step_rate, key_rows, query_rows, grad_out):
    tokens, channels = inputs.shape[1:]
    state_dim = key_rows.shape[2]
    num_blocks = tokens // BLOCK

    def to_blocks(array_in):
        return array_in[0].astype(jnp.float32).reshape(num_blocks, BLOCK, array_in.shape[2])

    def summarize(carried, block_in):
        x, rate, key_blk, query_blk, grad_blk = block_in
        keys_sq = key_blk * key_blk
        step = rate / (1.0 + rate * jnp.sum(keys_sq, axis=1)[:, None])
        decays = 1.0 - step[:, None, :] * keys_sq[:, :, None]
        drives = (step * x)[:, None, :] * key_blk[:, :, None]
        before = jnp.cumprod(decays, axis=0)
        suffix = jnp.cumprod(decays[::-1], axis=0)[::-1]
        after = jnp.concatenate([suffix[1:], jnp.ones_like(decays[:1])], axis=0)
        total = before[-1]
        end = jnp.sum(drives * after, axis=0)
        back = jnp.sum(grad_blk[:, None, :] * query_blk[:, :, None] * before, axis=0)
        return (
            carried[0] * total,
            total * carried[1] + end,
            carried[2] + carried[0] * back,
        ), None

    zero = jnp.zeros((state_dim, channels), jnp.float32)
    blocked = tuple(map(to_blocks, (inputs, step_rate, key_rows, query_rows, grad_out)))
    return lax.scan(summarize, (jnp.ones_like(zero), zero, zero), blocked)[0]


def spread_columns(matrix, table_ref):
    rows, tokens = matrix.shape
    for t in range(tokens):
        table_ref[t] = jnp.broadcast_to(matrix[:, t : t + 1], (rows, LANES))


def halves(value):
    return [value[at : at + SUB] for at in range(0, value.shape[0], SUB)]


def row(ref, tile, t):
    return ref[tile, pl.ds(t, SUB, stride=0), :]


def tile_at(j):
    return pl.ds(j * LANES, LANES)


def lane_sums(values):
    ones = jnp.ones((SUB, LANES), jnp.bfloat16)

    def product(part):
        return lax.dot_general(
            ones, part, (((1,), (1,)), ((), ())), preferred_element_type=jnp.float32
        )

    high = values.astype(jnp.bfloat16)
    low = (values - high.astype(jnp.float32)).astype(jnp.bfloat16)
    return product(high) + product(low)


def first_kernel(backwards, has_entry, has_tables, *refs):
    refs = list(refs)
    x_ref, rate_ref, key_ref, query_ref, go_ref = refs[:5]
    del refs[:5]
    entry_ref = refs.pop(0) if has_entry else None
    given = [refs.pop(0), refs.pop(0)] if has_tables else None
    path_ref, end_ref, step_ref, drive_ref, x32_ref, go32_ref, inverse_ref = refs[:7]
    keys_ref, queries_ref = given or refs[7:]
    states, tokens = key_ref.shape[1:]
    tiles = x_ref.shape[2] // LANES
    key = key_ref[0].astype(jnp.float32)
    if not has_tables:
        spread_columns(key, keys_ref)
        spread_columns(query_ref[0].astype(jnp.float32), queries_ref)
    key_norm = jnp.sum(key * key, axis=0, keepdims=True)
    norm = jnp.transpose(jnp.broadcast_to(key_norm, (LANES, tokens)))
    for j in range(tiles):
        rate = rate_ref[0, :, tile_at(j)]
        x = x_ref[0, :, tile_at(j)].astype(jnp.float32)
        inverse = 1.0 / (1.0 + rate * norm)
        step = rate * inverse
        inverse_ref[j, :tokens] = inverse
        step_ref[j, :tokens] = step
        x32_ref[j, :tokens] = x
        drive_ref[j, :tokens] = step * x
        go32_ref[j, :tokens] = go_ref[0, :, tile_at(j)].astype(jnp.float32)

    if has_entry:
        entry = [halves(entry_ref[:, tile_at(j)]) for j in range(tiles)]
    else:
        entry = [[jnp.zeros((SUB, LANES), jnp.float32)] * (states // SUB)] * tiles

    def finish(state):
        for j in range(tiles):
            end_ref[:, tile_at(j)] = jnp.concatenate(state[j], axis=0)

    def run_states():
        def block(b, state):
            base = b * UNROLL
            state = [list(part) for part in state]
            for u in range(UNROLL):
                k = halves(keys_ref[base + u])
                k2 = [part * part for part in k]
                for j in range(tiles):
                    step = row(step_ref, j, base + u)
                    drive = row(drive_ref, j, base + u)
                    for h in range(len(k)):
                        state[j][h] = (1.0 - step * k2[h]) * state[j][h] + drive * k[h]
                        path_ref[base + u, pl.ds(h * SUB, SUB), tile_at(j)] = state[j][h]
            return state

        finish(lax.fori_loop(0, tokens // UNROLL, block, entry))

    def run_grads():
        def block(i, state):
            base = tokens - UNROLL - i * UNROLL
            state = [list(part) for part in state]
            for u in reversed(range(UNROLL)):
                k2 = [part * part for part in halves(keys_ref[base + u])]
                q = halves(queries_ref[base + u])
                for j in range(tiles):
                    step = row(step_ref, j, base + u)
                    go = row(go32_ref, j, base + u)
                    for h in range(len(q)):
                        grad = go * q[h] + state[j][h]
                        path_ref[base + u, pl.ds(h * SUB, SUB), tile_at(j)] = grad
                        state[j][h] = (1.0 - step * k2[h]) * grad
            return state

        finish(lax.fori_loop(0, tokens // UNROLL, block, entry))

    choose(backwards, run_grads, run_states)


def choose(flag, if_set, if_not):
    if flag is None:
        group = lax.axis_index("ctx")
        pl.when(group != 0)(if_set)
        pl.when(group == 0)(if_not)
    else:
        (if_set if flag else if_not)()


def second_kernel(onwards_here, last, heads, has_start, has_before, *refs):
    refs = list(refs)
    key_ref, entry_ref, path_ref, step_ref, drive_ref, x32_ref, go32_ref, inverse_ref = refs[:8]
    keys_ref, queries_ref = refs[8:10]
    del refs[:10]
    start_ref = refs.pop(0) if has_start else None
    before_ref = refs.pop(0) if has_before else None
    message_refs = refs[:heads]
    sums_ref, dot_ref, weighted_ref, key_part_ref, query_part_ref, norm_ref = refs[heads:]
    states, tokens = key_ref.shape[1:]
    tiles = step_ref.shape[0]
    width = tiles * LANES
    key = key_ref[0].astype(jnp.float32)
    pair = range(states // SUB)

    def path_at(t, h, j):
        return path_ref[t, pl.ds(h * SUB, SUB), tile_at(j)]

    def step_through(back, advance):
        def block(i, state):
            base = tokens - UNROLL - i * UNROLL if back else i * UNROLL
            state = [list(part) for part in state]
            for u in reversed(range(UNROLL)) if back else range(UNROLL):
                t = base + u
                k, q = halves(keys_ref[t]), halves(queries_ref[t])
                k2 = [part * part for part in k]
                sums = None
                for j in range(tiles):
                    step, drive, go = (
                        row(ref, j, t) for ref in (step_ref, drive_ref, go32_ref)
                    )
                    dots, weights, terms = [], [], []
                    for h in pair:
                        decay = 1.0 - step * k2[h]
                        grad, here, previous, state[j][h] = advance(
                            t, u, h, j, state[j][h], decay, drive, go, k[h], q[h]
                        )
                        weight = grad * previous
                        dots.append(grad * k[h])
                        weights.append(weight * k2[h])
                        terms += [grad * drive, weight * step, here * go]
                    dot_ref[j, pl.ds(pl.multiple_of(t * SUB, SUB), SUB), :] = sum(dots[1:], dots[0])
                    weighted_ref[j, pl.ds(pl.multiple_of(t * SUB, SUB), SUB), :] = sum(
                        weights[1:], weights[0]
                    )
                    sums = terms if j == 0 else [a + b for a, b in zip(sums, terms)]
                for h in pair:
                    by_drive, by_decay, by_query = sums[3 * h : 3 * h + 3]
                    at = pl.ds(pl.multiple_of(t * states + h * SUB, SUB), SUB)
                    key_part_ref[at, :] = by_drive - (2.0 * k[h]) * by_decay
                    query_part_ref[at, :] = by_query
            return state

        entry = [halves(entry_ref[:, tile_at(j)]) for j in range(tiles)]
        lax.fori_loop(0, tokens // UNROLL, block, entry)

    def backwards(t, u, h, j, state, decay, drive, go, k, q):
        grad = go * q + state
        earlier = path_at(jnp.maximum(t - 1, 0), h, j)
        if u == 0:
            start = start_ref[pl.ds(h * SUB, SUB), tile_at(j)] if has_start else 0.0
            earlier = jnp.where(t == 0, start, earlier)
        return grad, path_at(t, h, j), earlier, decay * grad

    def onwards(t, u, h, j, state, decay, drive, go, k, q):
        here = decay * state + drive * k
        return path_at(t, h, j), here, state, here

    choose(onwards_here, lambda: step_through(False, onwards), lambda: step_through(True, backwards))

    part = tokens // heads
    rows = 2 * SUB
    position = lax.axis_index("head")
    for d in range(heads):
        for r in range(part // rows):
            base = pl.multiple_of((position ^ d) * part + r * rows, rows)
            to = pl.ds(r * rows, rows)
            norm_sum = None
            for j in range(tiles):
                dot, weighted = (
                    sum(ref[j, pl.ds(base * SUB + s, rows, stride=SUB), :] for s in range(SUB))
                    for ref in (dot_ref, weighted_ref)
                )
                step, x, inverse = (
                    ref[j, pl.ds(base, rows), :] for ref in (step_ref, x32_ref, inverse_ref)
                )
                grad_step = x * dot - weighted
                message_refs[d][to, tile_at(j)] = (step * dot).astype(jnp.bfloat16)
                message_refs[d][to, tile_at(tiles + j)] = (grad_step * inverse * inverse).astype(
                    jnp.bfloat16
                )
                term = grad_step * step * step
                norm_sum = term if j == 0 else norm_sum + term
            norm_ref[pl.ds(base, rows), :] = norm_sum
    norm_row = lane_sums(norm_ref[...])[:1]
    for n in range(states):
        at = pl.ds(n, tokens, stride=states)
        sums_ref[n : n + 1, :] = lane_sums(key_part_ref[at, :])[:1]
        sums_ref[states + n : states + n + 1, :] = lane_sums(query_part_ref[at, :])[:1]
    sums_ref[:states] = sums_ref[:states] - 2.0 * key * norm_row
    if has_before:
        sums_ref[...] = sums_ref[...] + before_ref[...]
    if last:
        quarters = 2 * states // SUB
        lane = lax.broadcasted_iota(jnp.int32, (SUB, tokens), 1) // part
        for d in range(heads):
            shift = (heads - (position ^ d)) * part
            packed = None
            for i in range(quarters):
                turned = pltpu.roll(
                    sums_ref[SUB * i : SUB * i + SUB], lax.rem(shift + i * part, tokens), 1
                )
                packed = turned if packed is None else jnp.where(lane == i, turned, packed)
            high = packed.astype(jnp.bfloat16).astype(jnp.float32)
            both = jnp.concatenate([high, packed - high], axis=0).astype(jnp.bfloat16)
            message_refs[d][:rows, pl.ds(2 * width, LANES)] = both
            message_refs[d][rows:, pl.ds(2 * width, LANES)] = jnp.zeros(
                (part - rows, LANES), jnp.bfloat16
            )


def gather_kernel(heads, chunks, *refs):
    pieces, (in_ref, rate_ref, key_ref, query_ref) = refs[:-4], refs[-4:]
    states, part = key_ref.shape[1:]
    channels = in_ref.shape[2] // heads
    width = channels // chunks
    position = lax.axis_index("head")
    total = None
    for c in range(chunks):
        for d in range(heads):
            piece = pieces[c * heads + d]
            at = pl.multiple_of((position ^ d) * channels + c * width, LANES)
            in_ref[0, :, pl.ds(at, width)] = piece[:, pl.ds(0, width)]
            rate_ref[0, :, pl.ds(at, width)] = piece[:, pl.ds(width, width)]
            if c == chunks - 1:
                both = piece[: 2 * SUB, pl.ds(2 * width, LANES)].astype(jnp.float32)
                both = both[:SUB] + both[SUB:]
                total = both if total is None else total + both
    for i in range(states // SUB):
        key_ref[0, SUB * i : SUB * i + SUB] = total[:, i * part : (i + 1) * part]
        at = states // SUB + i
        query_ref[0, SUB * i : SUB * i + SUB] = total[:, at * part : (at + 1) * part]


def shards(inputs, step_rate, key_rows, query_rows, grad_out):
    _, tokens, channels = inputs.shape
    states = key_rows.shape[2]
    heads = lax.axis_size("head")
    groups = lax.axis_size("ctx")
    width = channels // CHUNKS
    part = tokens // heads
    key_cols = jnp.swapaxes(key_rows, 1, 2)
    query_cols = jnp.swapaxes(query_rows, 1, 2)
    f32 = jnp.float32
    params = pltpu.CompilerParams(vmem_limit_bytes=VMEM_LIMIT)
    whole = pl.BlockSpec(memory_space=pltpu.VMEM)
    plane = pltpu.VMEM((width // LANES, tokens + SUB, LANES), f32)

    table = pltpu.VMEM((tokens, states, LANES), f32)

    def first(c, backwards, tables=(), entry=None):
        wide = pl.BlockSpec((1, tokens, width), lambda i: (0, 0, c))
        specs = [wide, wide, whole, whole, wide]
        arrays = [inputs, step_rate, key_cols, query_cols, grad_out]
        if c == 0:
            arrays = [pltpu.with_memory_space_constraint(a, pltpu.HBM) for a in arrays]
        extra = [*(() if entry is None else (entry,)), *tables]
        out_shape = [
            pltpu.VMEM((tokens, states, width), f32),
            jax.ShapeDtypeStruct((states, width), f32),
        ]
        out_shape += [plane] * 5 + [table] * (0 if tables else 2)
        path, end, *carried = pl.pallas_call(
            functools.partial(first_kernel, backwards, entry is not None, bool(tables)),
            grid=(1,),
            in_specs=specs + [whole] * len(extra),
            out_specs=[whole] * len(out_shape),
            out_shape=out_shape,
            compiler_params=params,
        )(*arrays, *extra)
        return path, end, carried[:5], tuple(tables) or tuple(carried[5:])

    def second(c, onwards_here, entry, carried, start, before):
        last = c == CHUNKS - 1
        wide_message = 2 * width + (LANES if last else 0)
        extra = [a for a in (start, before) if a is not None]
        parts = pltpu.VMEM((width // LANES, (tokens + 1) * SUB, LANES), f32)
        sums = pltpu.VMEM(((tokens + 1) * states, LANES), f32)
        piece = jax.ShapeDtypeStruct((part, wide_message), jnp.bfloat16)
        *pieces, sums = pl.pallas_call(
            functools.partial(
                second_kernel, onwards_here, last, heads, start is not None, before is not None
            ),
            in_specs=[whole] * (10 + len(extra)),
            out_specs=[whole] * (heads + 1),
            out_shape=[piece] * heads + [pltpu.VMEM((2 * states, tokens), f32)],
            scratch_shapes=[parts, parts, sums, sums, pltpu.VMEM((tokens, LANES), f32)],
            compiler_params=params,
        )(key_cols, entry, *carried, *extra)
        return pieces, sums

    work = []
    if groups == 2:
        here = None
        tables = ()
        for c in range(CHUNKS):
            path, end, carried, tables = first(c, here, tables)
            entry = lax.ppermute(end, "ctx", [(0, 1), (1, 0)])
            work.append((entry, [path, *carried, *tables], None))
    else:
        here = False
        product, end, back = group_summary(inputs, step_rate, key_rows, query_rows, grad_out)
        unit = (jnp.ones_like(product), jnp.zeros_like(product))
        starts = prefix((product, end), "ctx", unit, False)[1]
        entries = prefix((product, back), "ctx", unit, True)[1]
        tables = ()
        for c in range(CHUNKS):
            at = slice(c * width, (c + 1) * width)
            path, _, carried, tables = first(c, here, tables, starts[:, at])
            work.append((entries[:, at], [path, *carried, *tables], starts[:, at]))

    sums = None
    arrived = []
    for c, (entry, carried, start) in enumerate(work):
        pieces, sums = second(c, here, entry, carried, start, sums)
        arrived.append(pieces[0])
        for d in range(1, heads):
            arrived.append(lax.ppermute(pieces[d], "head", [(s, s ^ d) for s in range(heads)]))

    grad_in, grad_rate, grad_key, grad_query = pl.pallas_call(
        functools.partial(gather_kernel, heads, CHUNKS),
        in_specs=[whole] * len(arrived),
        out_specs=[whole] * 4,
        out_shape=[
            jax.ShapeDtypeStruct((1, part, heads * channels), jnp.bfloat16),
            jax.ShapeDtypeStruct((1, part, heads * channels), jnp.bfloat16),
            jax.ShapeDtypeStruct((1, states, part), f32),
            jax.ShapeDtypeStruct((1, states, part), f32),
        ],
        compiler_params=params,
    )(*arrived)
    return (grad_in, grad_rate, jnp.swapaxes(grad_key, 1, 2), jnp.swapaxes(grad_query, 1, 2))


def solution(mesh):
    placed = (
        P("dp", "ctx", "head"),
        P("dp", "ctx", "head"),
        P("dp", "ctx", None),
        P("dp", "ctx", None),
        P("dp", "ctx", "head"),
    )
    spread = P("dp", ("ctx", "head"), None)
    return jax.shard_map(
        shards, mesh=mesh, in_specs=placed, out_specs=(spread,) * 4, check_vma=False
    )
```

```python
import functools

import jax
import jax.numpy as jnp
from jax import lax
from jax.experimental import pallas as pl
from jax.experimental.pallas import tpu as pltpu
from jax.sharding import PartitionSpec as P

BLOCK = 16
LANES = 128
SUB = 8
UNROLL = 8
CHUNKS = 4
AHEAD = 1
VMEM_LIMIT = 20 * 1024 * 1024


def affine(earlier, subsequent):
    return (earlier[0] * subsequent[0], subsequent[0] * earlier[1] + subsequent[1])


def prefix(array, axis, identity, reverse):
    size, position = (lax.axis_size(axis), lax.axis_index(axis))
    everything = jax.tree.map(lambda part: lax.all_gather(part, axis), array)
    start = jax.tree.map(
        lambda part, zero: jnp.broadcast_to(jnp.asarray(zero, part.dtype), part.shape),
        array,
        identity,
    )

    def hop(k, before):
        at = size - 1 - k if reverse else k
        reached = at > position if reverse else at < position
        new = affine(before, jax.tree.map(lambda part: part[at], everything))
        return jax.tree.map(lambda a, b: jnp.where(reached, a, b), new, before)

    return lax.fori_loop(0, size, hop, start)


def group_summary(inputs, step_rate, key_rows, query_rows, grad_out):
    tokens, channels = inputs.shape[1:]
    state_dim = key_rows.shape[2]
    num_blocks = tokens // BLOCK

    def to_blocks(array_in):
        return array_in[0].astype(jnp.float32).reshape(num_blocks, BLOCK, array_in.shape[2])

    def summarize(carried, block_in):
        x, rate, key_blk, query_blk, grad_blk = block_in
        keys_sq = key_blk * key_blk
        step = rate / (1.0 + rate * jnp.sum(keys_sq, axis=1)[:, None])
        decays = 1.0 - step[:, None, :] * keys_sq[:, :, None]
        drives = (step * x)[:, None, :] * key_blk[:, :, None]
        before = jnp.cumprod(decays, axis=0)
        suffix = jnp.cumprod(decays[::-1], axis=0)[::-1]
        after = jnp.concatenate([suffix[1:], jnp.ones_like(decays[:1])], axis=0)
        total = before[-1]
        end = jnp.sum(drives * after, axis=0)
        back = jnp.sum(grad_blk[:, None, :] * query_blk[:, :, None] * before, axis=0)
        return (
            carried[0] * total,
            total * carried[1] + end,
            carried[2] + carried[0] * back,
        ), None

    zero = jnp.zeros((state_dim, channels), jnp.float32)
    blocked = tuple(map(to_blocks, (inputs, step_rate, key_rows, query_rows, grad_out)))
    return lax.scan(summarize, (jnp.ones_like(zero), zero, zero), blocked)[0]


def spread_columns(matrix, table_ref):
    rows, tokens = matrix.shape
    for t in range(tokens):
        table_ref[t] = jnp.broadcast_to(matrix[:, t : t + 1], (rows, LANES))


def halves(value):
    return [value[at : at + SUB] for at in range(0, value.shape[0], SUB)]


def row(ref, tile, t):
    return ref[tile, pl.ds(t, SUB, stride=0), :]


def tile_at(j):
    return pl.ds(j * LANES, LANES)


def lane_sums(values):
    ones = jnp.ones((SUB, LANES), jnp.bfloat16)

    def product(part):
        return lax.dot_general(
            ones, part, (((1,), (1,)), ((), ())), preferred_element_type=jnp.float32
        )

    high = values.astype(jnp.bfloat16)
    low = (values - high.astype(jnp.float32)).astype(jnp.bfloat16)
    return product(high) + product(low)


def first_kernel(backwards, has_entry, has_tables, has_earlier, *refs):
    refs = list(refs)
    x_ref, rate_ref, key_ref, query_ref, go_ref = refs[:5]
    del refs[:5]
    entry_ref = refs.pop(0) if has_entry else None
    given = [refs.pop(0), refs.pop(0)] if has_tables else None
    if has_earlier:
        del refs[0]
    path_ref, end_ref, step_ref, drive_ref, x32_ref, go32_ref, inverse_ref = refs[:7]
    keys_ref, queries_ref = given or refs[7:9]
    states, tokens = key_ref.shape[1:]
    tiles = x_ref.shape[2] // LANES
    key = key_ref[0].astype(jnp.float32)
    if not has_tables:
        refs[9][...] = key
        spread_columns(key, keys_ref)
        spread_columns(query_ref[0].astype(jnp.float32), queries_ref)
    key_norm = jnp.sum(key * key, axis=0, keepdims=True)
    norm = jnp.transpose(jnp.broadcast_to(key_norm, (LANES, tokens)))
    for j in range(tiles):
        rate = rate_ref[0, :, tile_at(j)]
        x = x_ref[0, :, tile_at(j)].astype(jnp.float32)
        inverse = 1.0 / (1.0 + rate * norm)
        step = rate * inverse
        inverse_ref[j, :tokens] = inverse
        step_ref[j, :tokens] = step
        x32_ref[j, :tokens] = x
        drive_ref[j, :tokens] = step * x
        go32_ref[j, :tokens] = go_ref[0, :, tile_at(j)].astype(jnp.float32)

    if has_entry:
        entry = [halves(entry_ref[:, tile_at(j)]) for j in range(tiles)]
    else:
        entry = [[jnp.zeros((SUB, LANES), jnp.float32)] * (states // SUB)] * tiles

    def finish(state):
        for j in range(tiles):
            end_ref[:, tile_at(j)] = jnp.concatenate(state[j], axis=0)

    def run_states():
        def block(b, state):
            base = b * UNROLL
            state = [list(part) for part in state]
            for u in range(UNROLL):
                k = halves(keys_ref[base + u])
                k2 = [part * part for part in k]
                for j in range(tiles):
                    step = row(step_ref, j, base + u)
                    drive = row(drive_ref, j, base + u)
                    for h in range(len(k)):
                        state[j][h] = (1.0 - step * k2[h]) * state[j][h] + drive * k[h]
                        path_ref[base + u, pl.ds(h * SUB, SUB), tile_at(j)] = state[j][h]
            return state

        finish(lax.fori_loop(0, tokens // UNROLL, block, entry))

    def run_grads():
        def block(i, state):
            base = tokens - UNROLL - i * UNROLL
            state = [list(part) for part in state]
            for u in reversed(range(UNROLL)):
                k2 = [part * part for part in halves(keys_ref[base + u])]
                q = halves(queries_ref[base + u])
                for j in range(tiles):
                    step = row(step_ref, j, base + u)
                    go = row(go32_ref, j, base + u)
                    for h in range(len(q)):
                        grad = go * q[h] + state[j][h]
                        path_ref[base + u, pl.ds(h * SUB, SUB), tile_at(j)] = grad
                        state[j][h] = (1.0 - step * k2[h]) * grad
            return state

        finish(lax.fori_loop(0, tokens // UNROLL, block, entry))

    choose(backwards, run_grads, run_states)


def choose(flag, if_set, if_not):
    if flag is None:
        group = lax.axis_index("ctx")
        pl.when(group != 0)(if_set)
        pl.when(group == 0)(if_not)
    else:
        (if_set if flag else if_not)()


def second_kernel(onwards_here, last, heads, has_start, has_before, *refs):
    refs = list(refs)
    entry_ref, path_ref, step_ref, drive_ref, x32_ref, go32_ref, inverse_ref = refs[:7]
    keys_ref, queries_ref = refs[7:9]
    del refs[:9]
    start_ref = refs.pop(0) if has_start else None
    before = [refs.pop(0) for _ in range(3)] if has_before else None
    key_ref = refs.pop(0) if last else None
    piece_refs = refs[:heads]
    key_part_ref, query_part_ref, norm_ref, dot_ref, weighted_ref = refs[heads : heads + 5]
    tokens, states = keys_ref.shape[:2]
    tiles = step_ref.shape[0]
    pair = range(states // SUB)

    def path_at(t, h, j):
        return path_ref[t, pl.ds(h * SUB, SUB), tile_at(j)]

    def step_through(back, advance):
        def block(i, state):
            base = tokens - UNROLL - i * UNROLL if back else i * UNROLL
            state = [list(part) for part in state]
            for u in reversed(range(UNROLL)) if back else range(UNROLL):
                t = base + u
                k, q = halves(keys_ref[t]), halves(queries_ref[t])
                k2 = [part * part for part in k]
                sums = None
                for j in range(tiles):
                    step, drive, go = (
                        row(ref, j, t) for ref in (step_ref, drive_ref, go32_ref)
                    )
                    dots, weights, terms = [], [], []
                    for h in pair:
                        decay = 1.0 - step * k2[h]
                        grad, here, previous, state[j][h] = advance(
                            t, u, h, j, state[j][h], decay, drive, go, k[h], q[h]
                        )
                        weight = grad * previous
                        dots.append(grad * k[h])
                        weights.append(weight * k2[h])
                        terms += [grad * drive, weight * step, here * go]
                    dot_ref[j, pl.ds(pl.multiple_of(t * SUB, SUB), SUB), :] = sum(dots[1:], dots[0])
                    weighted_ref[j, pl.ds(pl.multiple_of(t * SUB, SUB), SUB), :] = sum(
                        weights[1:], weights[0]
                    )
                    sums = terms if j == 0 else [a + b for a, b in zip(sums, terms)]
                for h in pair:
                    by_drive, by_decay, by_query = sums[3 * h : 3 * h + 3]
                    at = pl.ds(pl.multiple_of(t * states + h * SUB, SUB), SUB)
                    by_key = by_drive - (2.0 * k[h]) * by_decay
                    if has_before:
                        by_key = by_key + before[0][at, :]
                        by_query = by_query + before[1][at, :]
                    key_part_ref[at, :] = by_key
                    query_part_ref[at, :] = by_query
            return state

        entry = [halves(entry_ref[:, tile_at(j)]) for j in range(tiles)]
        lax.fori_loop(0, tokens // UNROLL, block, entry)

    def backwards(t, u, h, j, state, decay, drive, go, k, q):
        grad = go * q + state
        earlier = path_at(jnp.maximum(t - 1, 0), h, j)
        if u == 0:
            start = start_ref[pl.ds(h * SUB, SUB), tile_at(j)] if has_start else 0.0
            earlier = jnp.where(t == 0, start, earlier)
        return grad, path_at(t, h, j), earlier, decay * grad

    def onwards(t, u, h, j, state, decay, drive, go, k, q):
        here = decay * state + drive * k
        return path_at(t, h, j), here, state, here

    choose(onwards_here, lambda: step_through(False, onwards), lambda: step_through(True, backwards))

    part = tokens // heads
    rows = 2 * SUB
    position = lax.axis_index("head")
    for d in range(heads):
        for r in range(part // rows):
            base = pl.multiple_of((position ^ d) * part + r * rows, rows)
            norm_sum = before[2][pl.ds(base, rows), :] if has_before else None
            for j in range(tiles):
                dot, weighted = (
                    sum(ref[j, pl.ds(base * SUB + s, rows, stride=SUB), :] for s in range(SUB))
                    for ref in (dot_ref, weighted_ref)
                )
                step, x, inverse = (
                    ref[j, pl.ds(base, rows), :] for ref in (step_ref, x32_ref, inverse_ref)
                )
                grad_step = x * dot - weighted
                grad_rate = grad_step * inverse * inverse
                to = j * part + r * rows
                piece_refs[d][pl.ds(to, rows), :] = (step * dot).astype(jnp.bfloat16)
                to += tiles * part
                piece_refs[d][pl.ds(to, rows), :] = grad_rate.astype(jnp.bfloat16)
                term = grad_step * step * step
                norm_sum = term if norm_sum is None else norm_sum + term
            norm_ref[pl.ds(base, rows), :] = norm_sum
    if not last:
        return

    key = key_ref[...]
    norm_row = lane_sums(norm_ref[...])[:1]
    sums_ref = refs[heads + 5]
    for n in range(states):
        at = pl.ds(n, tokens, stride=states)
        sums_ref[n : n + 1, :] = lane_sums(key_part_ref[at, :])[:1]
        sums_ref[states + n : states + n + 1, :] = lane_sums(query_part_ref[at, :])[:1]
    sums_ref[:states] = sums_ref[:states] - 2.0 * key * norm_row
    quarters = 2 * states // SUB
    lane = lax.broadcasted_iota(jnp.int32, (SUB, tokens), 1) // part
    for d in range(heads):
        shift = (heads - (position ^ d)) * part
        packed = None
        for i in range(quarters):
            turned = pltpu.roll(
                sums_ref[SUB * i : SUB * i + SUB], lax.rem(shift + i * part, tokens), 1
            )
            packed = turned if packed is None else jnp.where(lane == i, turned, packed)
        high = packed.astype(jnp.bfloat16).astype(jnp.float32)
        both = jnp.concatenate([high, packed - high], axis=0).astype(jnp.bfloat16)
        piece_refs[d][pl.ds(2 * tiles * part, rows), :] = both


def gather_kernel(heads, chunks, *refs):
    pieces, (in_ref, rate_ref, key_ref, query_ref) = refs[:-4], refs[-4:]
    states, part = key_ref.shape[1:]
    channels = in_ref.shape[2] // heads
    width = channels // chunks
    position = lax.axis_index("head")
    tiles = width // LANES
    total = None
    for c in range(chunks):
        for d in range(heads):
            piece = pieces[c * heads + d]
            at = pl.multiple_of((position ^ d) * channels + c * width, LANES)
            for j in range(tiles):
                to = pl.ds(at + j * LANES, LANES)
                in_ref[0, :, to] = piece[pl.ds(j * part, part), :]
                rate_ref[0, :, to] = piece[pl.ds((tiles + j) * part, part), :]
            if c == chunks - 1:
                both = piece[pl.ds(2 * tiles * part, 2 * SUB), :].astype(jnp.float32)
                both = both[:SUB] + both[SUB:]
                total = both if total is None else total + both
    for i in range(states // SUB):
        key_ref[0, SUB * i : SUB * i + SUB] = total[:, i * part : (i + 1) * part]
        at = states // SUB + i
        query_ref[0, SUB * i : SUB * i + SUB] = total[:, at * part : (at + 1) * part]


def shards(inputs, step_rate, key_rows, query_rows, grad_out):
    _, tokens, channels = inputs.shape
    states = key_rows.shape[2]
    heads = lax.axis_size("head")
    groups = lax.axis_size("ctx")
    width = channels // CHUNKS
    part = tokens // heads
    key_cols = jnp.swapaxes(key_rows, 1, 2)
    query_cols = jnp.swapaxes(query_rows, 1, 2)
    f32 = jnp.float32
    params = pltpu.CompilerParams(vmem_limit_bytes=VMEM_LIMIT)
    whole = pl.BlockSpec(memory_space=pltpu.VMEM)
    plane = pltpu.VMEM((width // LANES, tokens + SUB, LANES), f32)

    table = pltpu.VMEM((tokens, states, LANES), f32)

    def cost(passes):
        elements = tokens * states * width
        return pl.CostEstimate(flops=passes * elements, bytes_accessed=4 * elements, transcendentals=0)

    def first(c, backwards, tables=(), entry=None, earlier=None):
        wide = pl.BlockSpec((1, tokens, width), lambda i: (0, 0, c))
        specs = [wide, wide, whole, whole, wide]
        arrays = [inputs, step_rate, key_cols, query_cols, grad_out]
        if c == 0:
            arrays = [pltpu.with_memory_space_constraint(a, pltpu.HBM) for a in arrays]
        for a in (entry, *tables[:2]):
            if a is not None:
                specs, arrays = specs + [whole], arrays + [a]
        if earlier is not None:
            specs, arrays = specs + [pl.BlockSpec(memory_space=pl.ANY)], arrays + [earlier]
        out_shape = [
            pltpu.VMEM((tokens, states, width), f32),
            jax.ShapeDtypeStruct((states, width), f32),
        ]
        out_shape += [plane] * 5
        if not tables:
            out_shape += [table] * 2 + [pltpu.VMEM((states, tokens), f32)]
        path, end, *carried = pl.pallas_call(
            functools.partial(
                first_kernel, backwards, entry is not None, bool(tables), earlier is not None
            ),
            grid=(1,),
            in_specs=specs,
            out_specs=[whole] * len(out_shape),
            out_shape=out_shape,
            compiler_params=params,
            cost_estimate=cost(5),
        )(*arrays)
        return path, end, carried[:5], tuple(tables) or tuple(carried[5:])

    def second(c, onwards_here, entry, carried, tables, start, before):
        last = c == CHUNKS - 1
        keys, queries, key = tables
        extra = [*(() if start is None else (start,)), *before, *((key,) if last else ())]
        parts = pltpu.VMEM((width // LANES, (tokens + 1) * SUB, LANES), f32)
        sums = pltpu.VMEM(((tokens + 1) * states, LANES), f32)
        size = 2 * part * width // LANES + (2 * SUB if last else 0)
        piece = jax.ShapeDtypeStruct((size, LANES), jnp.bfloat16)
        results = pl.pallas_call(
            functools.partial(
                second_kernel, onwards_here, last, heads, start is not None, bool(before)
            ),
            in_specs=[whole] * (9 + len(extra)),
            out_specs=[whole] * (heads + 3),
            out_shape=[piece] * heads + [sums, sums, pltpu.VMEM((tokens, LANES), f32)],
            scratch_shapes=[parts, parts] + [pltpu.VMEM((2 * states, tokens), f32)] * last,
            compiler_params=params,
            cost_estimate=cost(20),
        )(entry, *carried, keys, queries, *extra)
        return results[:heads], results[heads:]

    entries = starts = None
    here = None
    if groups != 2:
        here = False
        product, end, back = group_summary(inputs, step_rate, key_rows, query_rows, grad_out)
        unit = (jnp.ones_like(product), jnp.zeros_like(product))
        starts = prefix((product, end), "ctx", unit, False)[1]
        entries = prefix((product, back), "ctx", unit, True)[1]

    def part_of(array, c):
        return None if array is None else array[:, c * width : (c + 1) * width]

    tables, before, work, arrived = (), (), [], []
    for c in range(CHUNKS + AHEAD):
        if c < CHUNKS:
            earlier = before[2] if before else None
            path, end, carried, tables = first(c, here, tables, part_of(starts, c), earlier)
            entry = part_of(entries, c)
            if entry is None:
                entry = lax.ppermute(end, "ctx", [(0, 1), (1, 0)])
            work.append((entry, [path, *carried], part_of(starts, c)))
        if c >= AHEAD:
            entry, carried, start = work[c - AHEAD]
            pieces, before = second(c - AHEAD, here, entry, carried, tables, start, before)
            arrived.append(pieces[0])
            for d in range(1, heads):
                arrived.append(lax.ppermute(pieces[d], "head", [(s, s ^ d) for s in range(heads)]))

    grad_in, grad_rate, grad_key, grad_query = pl.pallas_call(
        functools.partial(gather_kernel, heads, CHUNKS),
        in_specs=[whole] * len(arrived),
        out_specs=[whole] * 4,
        out_shape=[
            jax.ShapeDtypeStruct((1, part, heads * channels), jnp.bfloat16),
            jax.ShapeDtypeStruct((1, part, heads * channels), jnp.bfloat16),
            jax.ShapeDtypeStruct((1, states, part), f32),
            jax.ShapeDtypeStruct((1, states, part), f32),
        ],
        compiler_params=params,
    )(*arrived)
    return (grad_in, grad_rate, jnp.swapaxes(grad_key, 1, 2), jnp.swapaxes(grad_query, 1, 2))


def solution(mesh):
    placed = (
        P("dp", "ctx", "head"),
        P("dp", "ctx", "head"),
        P("dp", "ctx", None),
        P("dp", "ctx", None),
        P("dp", "ctx", "head"),
    )
    spread = P("dp", ("ctx", "head"), None)
    return jax.shard_map(
        shards, mesh=mesh, in_specs=placed, out_specs=(spread,) * 4, check_vma=False
    )
```

```python
import functools

import jax
import jax.numpy as jnp
from jax import lax
from jax.experimental import pallas as pl
from jax.experimental.pallas import tpu as pltpu
from jax.sharding import PartitionSpec as P

BLOCK = 16
LANES = 128
SUB = 8
UNROLL = 8
FIRST_TILES = 5
DELAYED = (1,)
VMEM_LIMIT = 20 * 1024 * 1024


def affine(earlier, subsequent):
    return (earlier[0] * subsequent[0], subsequent[0] * earlier[1] + subsequent[1])


def prefix(array, axis, identity, reverse):
    size, position = (lax.axis_size(axis), lax.axis_index(axis))
    everything = jax.tree.map(lambda part: lax.all_gather(part, axis), array)
    start = jax.tree.map(
        lambda part, zero: jnp.broadcast_to(jnp.asarray(zero, part.dtype), part.shape),
        array,
        identity,
    )

    def hop(k, before):
        at = size - 1 - k if reverse else k
        reached = at > position if reverse else at < position
        new = affine(before, jax.tree.map(lambda part: part[at], everything))
        return jax.tree.map(lambda a, b: jnp.where(reached, a, b), new, before)

    return lax.fori_loop(0, size, hop, start)


def group_summary(inputs, step_rate, key_rows, query_rows, grad_out):
    tokens, channels = inputs.shape[1:]
    state_dim = key_rows.shape[2]
    num_blocks = tokens // BLOCK

    def to_blocks(array_in):
        return array_in[0].astype(jnp.float32).reshape(num_blocks, BLOCK, array_in.shape[2])

    def summarize(carried, block_in):
        x, rate, key_blk, query_blk, grad_blk = block_in
        keys_sq = key_blk * key_blk
        step = rate / (1.0 + rate * jnp.sum(keys_sq, axis=1)[:, None])
        decays = 1.0 - step[:, None, :] * keys_sq[:, :, None]
        drives = (step * x)[:, None, :] * key_blk[:, :, None]
        before = jnp.cumprod(decays, axis=0)
        suffix = jnp.cumprod(decays[::-1], axis=0)[::-1]
        after = jnp.concatenate([suffix[1:], jnp.ones_like(decays[:1])], axis=0)
        total = before[-1]
        end = jnp.sum(drives * after, axis=0)
        back = jnp.sum(grad_blk[:, None, :] * query_blk[:, :, None] * before, axis=0)
        return (
            carried[0] * total,
            total * carried[1] + end,
            carried[2] + carried[0] * back,
        ), None

    zero = jnp.zeros((state_dim, channels), jnp.float32)
    blocked = tuple(map(to_blocks, (inputs, step_rate, key_rows, query_rows, grad_out)))
    return lax.scan(summarize, (jnp.ones_like(zero), zero, zero), blocked)[0]


def spread_columns(matrix, table_ref):
    rows, tokens = matrix.shape
    for t in range(tokens):
        table_ref[t] = jnp.broadcast_to(matrix[:, t : t + 1], (rows, LANES))


def halves(value):
    return [value[at : at + SUB] for at in range(0, value.shape[0], SUB)]


def row(ref, tile, t):
    return ref[tile, pl.ds(t, SUB, stride=0), :]


def tile_at(j):
    return pl.ds(j * LANES, LANES)


def lane_sums(values):
    high = values.astype(jnp.bfloat16)
    low = (values - high.astype(jnp.float32)).astype(jnp.bfloat16)
    both = jnp.concatenate([high, low], axis=1)
    ones = jnp.ones((2 * LANES, LANES), jnp.bfloat16)
    return jnp.dot(both, ones, preferred_element_type=jnp.float32)


def first_kernel(offset, width, backwards, has_entry, has_tables, *refs):
    refs = list(refs)
    x_ref, rate_ref, key_ref, query_ref, go_ref = refs[:5]
    del refs[:5]
    entry_ref = refs.pop(0) if has_entry else None
    given = [refs.pop(0), refs.pop(0)] if has_tables else None
    path_ref, end_ref, step_ref, drive_ref, x32_ref, go32_ref, inverse_ref = refs[:7]
    keys_ref, queries_ref = given or refs[7:9]
    states, tokens = key_ref.shape[1:]
    tiles = width // LANES
    key = key_ref[0].astype(jnp.float32)
    if not has_tables:
        refs[9][...] = key
        spread_columns(key, keys_ref)
        spread_columns(query_ref[0].astype(jnp.float32), queries_ref)
    key_norm = jnp.sum(key * key, axis=0, keepdims=True)
    norm = jnp.transpose(jnp.broadcast_to(key_norm, (LANES, tokens)))
    for j in range(tiles):
        at = pl.ds(offset + j * LANES, LANES)
        rate = rate_ref[0, :, at]
        x = x_ref[0, :, at].astype(jnp.float32)
        inverse = 1.0 / (1.0 + rate * norm)
        step = rate * inverse
        inverse_ref[j, :tokens] = inverse
        step_ref[j, :tokens] = step
        x32_ref[j, :tokens] = x
        drive_ref[j, :tokens] = step * x
        go32_ref[j, :tokens] = go_ref[0, :, at].astype(jnp.float32)

    if has_entry:
        entry = [halves(entry_ref[:, tile_at(j)]) for j in range(tiles)]
    else:
        entry = [[jnp.zeros((SUB, LANES), jnp.float32)] * (states // SUB)] * tiles

    def finish(state):
        for j in range(tiles):
            end_ref[:, tile_at(j)] = jnp.concatenate(state[j], axis=0)

    def run_states():
        def block(b, state):
            base = b * UNROLL
            state = [list(part) for part in state]
            for u in range(UNROLL):
                k = halves(keys_ref[base + u])
                k2 = [part * part for part in k]
                for j in range(tiles):
                    step = row(step_ref, j, base + u)
                    drive = row(drive_ref, j, base + u)
                    for h in range(len(k)):
                        state[j][h] = (1.0 - step * k2[h]) * state[j][h] + drive * k[h]
                        path_ref[base + u, pl.ds(h * SUB, SUB), tile_at(j)] = state[j][h]
            return state

        finish(lax.fori_loop(0, tokens // UNROLL, block, entry))

    def run_grads():
        def block(i, state):
            base = tokens - UNROLL - i * UNROLL
            state = [list(part) for part in state]
            for u in reversed(range(UNROLL)):
                k2 = [part * part for part in halves(keys_ref[base + u])]
                q = halves(queries_ref[base + u])
                for j in range(tiles):
                    step = row(step_ref, j, base + u)
                    go = row(go32_ref, j, base + u)
                    for h in range(len(q)):
                        grad = go * q[h] + state[j][h]
                        path_ref[base + u, pl.ds(h * SUB, SUB), tile_at(j)] = grad
                        state[j][h] = (1.0 - step * k2[h]) * grad
            return state

        finish(lax.fori_loop(0, tokens // UNROLL, block, entry))

    choose(backwards, run_grads, run_states)


def choose(flag, if_set, if_not):
    if flag is None:
        group = lax.axis_index("ctx")
        pl.when(group != 0)(if_set)
        pl.when(group == 0)(if_not)
    else:
        (if_set if flag else if_not)()


def second_kernel(onwards_here, last, heads, has_start, *refs):
    refs = list(refs)
    entry_ref, path_ref, step_ref, drive_ref, x32_ref, go32_ref, inverse_ref = refs[:7]
    keys_ref, queries_ref = refs[7:9]
    del refs[:9]
    start_ref = refs.pop(0) if has_start else None
    before = [refs.pop(0) for _ in range(3)] if last else None
    key_ref = refs.pop(0) if last else None
    if not last:
        del refs[0]
    piece_refs = refs[:heads]
    key_part_ref, query_part_ref, norm_ref, dot_ref, weighted_ref = refs[heads : heads + 5]
    tokens, states = keys_ref.shape[:2]
    tiles = step_ref.shape[0]
    pair = range(states // SUB)

    def path_at(t, h, j):
        return path_ref[t, pl.ds(h * SUB, SUB), tile_at(j)]

    def step_through(back, advance):
        def block(i, state):
            base = tokens - UNROLL - i * UNROLL if back else i * UNROLL
            state = [list(part) for part in state]
            for u in reversed(range(UNROLL)) if back else range(UNROLL):
                t = base + u
                k, q = halves(keys_ref[t]), halves(queries_ref[t])
                k2 = [part * part for part in k]
                sums = None
                for j in range(tiles):
                    step, drive, go = (
                        row(ref, j, t) for ref in (step_ref, drive_ref, go32_ref)
                    )
                    dots, weights, terms = [], [], []
                    for h in pair:
                        decay = 1.0 - step * k2[h]
                        grad, here, previous, state[j][h] = advance(
                            t, u, h, j, state[j][h], decay, drive, go, k[h], q[h]
                        )
                        weight = grad * previous
                        dots.append(grad * k[h])
                        weights.append(weight * k2[h])
                        terms += [grad * drive, weight * step, here * go]
                    dot_ref[j, pl.ds(pl.multiple_of(t * SUB, SUB), SUB), :] = sum(dots[1:], dots[0])
                    weighted_ref[j, pl.ds(pl.multiple_of(t * SUB, SUB), SUB), :] = sum(
                        weights[1:], weights[0]
                    )
                    sums = terms if j == 0 else [a + b for a, b in zip(sums, terms)]
                for h in pair:
                    by_drive, by_decay, by_query = sums[3 * h : 3 * h + 3]
                    at = pl.ds(pl.multiple_of(t * states + h * SUB, SUB), SUB)
                    by_key = by_drive - (2.0 * k[h]) * by_decay
                    if last:
                        by_key = by_key + before[0][at, :]
                        by_query = by_query + before[1][at, :]
                    key_part_ref[at, :] = by_key
                    query_part_ref[at, :] = by_query
            return state

        entry = [halves(entry_ref[:, tile_at(j)]) for j in range(tiles)]
        lax.fori_loop(0, tokens // UNROLL, block, entry)

    def backwards(t, u, h, j, state, decay, drive, go, k, q):
        grad = go * q + state
        earlier = path_at(jnp.maximum(t - 1, 0), h, j)
        if u == 0:
            start = start_ref[pl.ds(h * SUB, SUB), tile_at(j)] if has_start else 0.0
            earlier = jnp.where(t == 0, start, earlier)
        return grad, path_at(t, h, j), earlier, decay * grad

    def onwards(t, u, h, j, state, decay, drive, go, k, q):
        here = decay * state + drive * k
        return path_at(t, h, j), here, state, here

    choose(onwards_here, lambda: step_through(False, onwards), lambda: step_through(True, backwards))

    part = tokens // heads
    rows = 2 * SUB
    position = lax.axis_index("head")
    width = tiles * LANES
    for d in range(heads):
        for r in range(part // rows):
            base = pl.multiple_of((position ^ d) * part + r * rows, rows)
            norm_sum = before[2][pl.ds(base, rows), :] if last else None
            for j in range(tiles):
                dot, weighted = (
                    sum(ref[j, pl.ds(base * SUB + s, rows, stride=SUB), :] for s in range(SUB))
                    for ref in (dot_ref, weighted_ref)
                )
                step, x, inverse = (
                    ref[j, pl.ds(base, rows), :] for ref in (step_ref, x32_ref, inverse_ref)
                )
                grad_step = x * dot - weighted
                grad_rate = grad_step * inverse * inverse
                to = j * LANES
                piece_refs[d][pl.ds(r * rows, rows), pl.ds(to, LANES)] = (step * dot).astype(
                    jnp.bfloat16
                )
                to += width
                piece_refs[d][pl.ds(r * rows, rows), pl.ds(to, LANES)] = grad_rate.astype(
                    jnp.bfloat16
                )
                term = grad_step * step * step
                norm_sum = term if norm_sum is None else norm_sum + term
            norm_ref[pl.ds(base, rows), :] = norm_sum
    if not last:
        return

    key = key_ref[...]
    lane = lax.broadcasted_iota(jnp.int32, (tokens, tokens), 1)
    own_row = lane == lax.broadcasted_iota(jnp.int32, (tokens, tokens), 0)
    norm_sums = jnp.where(own_row, lane_sums(norm_ref[...]), 0.0)
    norm_row = jnp.sum(norm_sums, axis=0, keepdims=True)
    lane = lax.broadcasted_iota(jnp.int32, (states, tokens), 1)
    totals = []
    for ref in (key_part_ref, query_part_ref):
        total = jnp.zeros((states, tokens), jnp.float32)
        for b in range(tokens // UNROLL):
            sums = lane_sums(ref[pl.ds(b * UNROLL * states, UNROLL * states), :])
            for u in range(UNROLL):
                total = jnp.where(
                    lane == b * UNROLL + u, sums[u * states : (u + 1) * states], total
                )
        totals.append(total)
    sums_ref = refs[heads + 5]
    sums_ref[:states] = totals[0] - 2.0 * key * norm_row
    sums_ref[states:] = totals[1]
    quarters = 2 * states // SUB
    lane = lax.broadcasted_iota(jnp.int32, (SUB, tokens), 1) // part
    for d in range(heads):
        shift = (heads - (position ^ d)) * part
        packed = None
        for i in range(quarters):
            turned = pltpu.roll(
                sums_ref[SUB * i : SUB * i + SUB], lax.rem(shift + i * part, tokens), 1
            )
            packed = turned if packed is None else jnp.where(lane == i, turned, packed)
        high = packed.astype(jnp.bfloat16).astype(jnp.float32)
        both = jnp.concatenate([high, packed - high], axis=0).astype(jnp.bfloat16)
        tail = pl.ds(2 * width, LANES)
        piece_refs[d][:rows, tail] = both
        piece_refs[d][rows:, tail] = jnp.zeros((part - rows, LANES), jnp.bfloat16)


def place(out_refs, piece, d, offset, width, channels, semaphores):
    at = pl.multiple_of((lax.axis_index("head") ^ d) * channels + offset, LANES)
    copies = []
    for i, out in enumerate(out_refs):
        copies.append(
            pltpu.make_async_copy(
                piece.at[:, pl.ds(i * width, width)],
                out.at[0, :, pl.ds(at, width)],
                semaphores.at[i],
            )
        )
        copies[-1].start()
    return copies


def early_kernel(distances, channels, *refs):
    pieces, out_refs, semaphores = refs[:-3], refs[-3:-1], refs[-1]
    width = pieces[0].shape[1] // 2
    copies = []
    for piece, d in zip(pieces, distances):
        copies += place(out_refs, piece, d, 0, width, channels, semaphores.at[d])
    for copy in copies:
        copy.wait()


def late_kernel(heads, distances, channels, *refs):
    pieces = refs[:heads][::-1]
    others = refs[heads : heads + len(distances)]
    *out_refs, key_ref, query_ref, semaphores = refs[heads + len(distances) + 2 :]
    states, part = key_ref.shape[1:]
    width = (pieces[0].shape[1] - LANES) // 2
    copies = []
    for d in range(heads):
        copies += place(
            out_refs, pieces[d], d, channels - width, width, channels, semaphores.at[d]
        )
    for i, d in enumerate(distances):
        copies += place(
            out_refs, others[i], d, 0, channels - width, channels, semaphores.at[heads + i]
        )
    total = None
    for d in range(heads):
        tail = pl.ds(2 * width, LANES)
        both = pieces[d][: 2 * SUB, tail].astype(jnp.float32)
        both = both[:SUB] + both[SUB:]
        total = both if total is None else total + both
    for i in range(states // SUB):
        key_ref[0, SUB * i : SUB * i + SUB] = total[:, i * part : (i + 1) * part]
        at = states // SUB + i
        query_ref[0, SUB * i : SUB * i + SUB] = total[:, at * part : (at + 1) * part]
    for copy in copies:
        copy.wait()


def shards(inputs, step_rate, key_rows, query_rows, grad_out):
    _, tokens, channels = inputs.shape
    states = key_rows.shape[2]
    heads = lax.axis_size("head")
    groups = lax.axis_size("ctx")
    part = tokens // heads
    tiles = channels // LANES
    first_width = tiles * FIRST_TILES // 8 * LANES
    widths = (first_width, channels - first_width)
    key_cols = jnp.swapaxes(key_rows, 1, 2)
    query_cols = jnp.swapaxes(query_rows, 1, 2)
    f32 = jnp.float32
    bf16 = jnp.bfloat16
    params = pltpu.CompilerParams(vmem_limit_bytes=VMEM_LIMIT)
    whole = pl.BlockSpec(memory_space=pltpu.VMEM)
    anywhere = pl.BlockSpec(memory_space=pl.ANY)
    table = pltpu.VMEM((tokens, states, LANES), f32)

    def cost(width, passes):
        elements = tokens * states * width
        return pl.CostEstimate(
            flops=passes * elements, bytes_accessed=4 * elements, transcendentals=0
        )

    def first(c, backwards, tables=(), entry=None):
        width = widths[c]
        arrays = [inputs, step_rate, key_cols, query_cols, grad_out]
        specs = [whole] * 5
        if c == 0:
            wide = pl.BlockSpec((1, tokens, width), lambda i: (0, 0, 0))
            specs = [wide, wide, whole, whole, wide]
            arrays = [pltpu.with_memory_space_constraint(a, pltpu.HBM) for a in arrays]
        extra = [*(() if entry is None else (entry,)), *tables[:2]]
        out_shape = [
            pltpu.VMEM((tokens, states, width), f32),
            jax.ShapeDtypeStruct((states, width), f32),
        ]
        out_shape += [pltpu.VMEM((width // LANES, tokens + SUB, LANES), f32)] * 5
        if not tables:
            out_shape += [table] * 2 + [pltpu.VMEM((states, tokens), f32)]
        path, end, *carried = pl.pallas_call(
            functools.partial(
                first_kernel, sum(widths[:c]), width, backwards, entry is not None, bool(tables)
            ),
            grid=(1,),
            in_specs=specs + [whole] * len(extra),
            out_specs=[whole] * len(out_shape),
            out_shape=out_shape,
            compiler_params=params,
            cost_estimate=cost(width, 5),
        )(*arrays, *extra)
        return path, end, carried[:5], tuple(tables) or tuple(carried[5:])

    def second(c, onwards_here, entry, carried, tables, start, before):
        width = widths[c]
        last = c == 1
        keys, queries, key = tables
        extra = [*(() if start is None else (start,)), *before, *((key,) if last else ())]
        specs = [whole] * (9 + len(extra))
        if not last:
            extra, specs = extra + [work[1][1][0]], specs + [anywhere]
        parts = pltpu.VMEM((width // LANES, (tokens + 1) * SUB, LANES), f32)
        sums = pltpu.VMEM(((tokens + 1) * states, LANES), f32)
        pieces = [jax.ShapeDtypeStruct((part, 2 * width + LANES * last), bf16)] * heads
        results = pl.pallas_call(
            functools.partial(second_kernel, onwards_here, last, heads, start is not None),
            in_specs=specs,
            out_specs=[whole] * (heads + 3),
            out_shape=pieces + [sums, sums, pltpu.VMEM((tokens, LANES), f32)],
            scratch_shapes=[parts, parts] + [pltpu.VMEM((2 * states, tokens), f32)] * last,
            compiler_params=params,
            cost_estimate=cost(width, 20),
        )(entry, *carried, keys, queries, *extra)
        return results[:heads], results[heads:]

    entries = starts = here = None
    if groups != 2:
        here = False
        product, end, back = group_summary(inputs, step_rate, key_rows, query_rows, grad_out)
        unit = (jnp.ones_like(product), jnp.zeros_like(product))
        starts = prefix((product, end), "ctx", unit, False)[1]
        entries = prefix((product, back), "ctx", unit, True)[1]

    def part_of(array, c):
        return None if array is None else array[:, sum(widths[:c]) : sum(widths[: c + 1])]

    def send(piece, d):
        return lax.ppermute(piece, "head", [(s, s ^ d) for s in range(heads)])

    tables, work = (), []
    for c in range(2):
        path, end, carried, tables = first(c, here, tables, part_of(starts, c))
        entry = part_of(entries, c)
        if entry is None:
            entry = lax.ppermute(end, "ctx", [(0, 1), (1, 0)])
        work.append((entry, [path, *carried], part_of(starts, c)))

    def call_second(c, before):
        entry, carried, start = work[c]
        return second(c, here, entry, carried, tables, start, before)

    away = list(range(heads - 1, 0, -1))
    pieces, before = call_second(0, ())
    arrived = {d: send(pieces[d], d) for d in away}
    arrived[0] = pieces[0]
    early = [d for d in range(heads) if d not in DELAYED]
    pieces, _ = call_second(1, before)
    late = {d: send(pieces[d], d) for d in away}
    late[0] = pieces[0]

    out = [jax.ShapeDtypeStruct((1, part, heads * channels), bf16)] * 2
    outs = pl.pallas_call(
        functools.partial(early_kernel, early, channels),
        in_specs=[whole] * len(early),
        out_specs=[anywhere] * 2,
        out_shape=out,
        scratch_shapes=[pltpu.SemaphoreType.DMA((heads, 2))],
        compiler_params=params,
    )(*[arrived[d] for d in early])
    pieces = [late[d] for d in reversed(range(heads))] + [arrived[d] for d in DELAYED]
    grad_in, grad_rate, grad_key, grad_query = pl.pallas_call(
        functools.partial(late_kernel, heads, DELAYED, channels),
        in_specs=[whole] * len(pieces) + [anywhere] * 2,
        out_specs=[anywhere] * 2 + [whole] * 2,
        out_shape=out + [jax.ShapeDtypeStruct((1, states, part), f32)] * 2,
        scratch_shapes=[pltpu.SemaphoreType.DMA((heads + len(DELAYED), 2))],
        input_output_aliases={len(pieces): 0, len(pieces) + 1: 1},
        compiler_params=params,
    )(*pieces, *outs)
    return (grad_in, grad_rate, jnp.swapaxes(grad_key, 1, 2), jnp.swapaxes(grad_query, 1, 2))


def solution(mesh):
    placed = (
        P("dp", "ctx", "head"),
        P("dp", "ctx", "head"),
        P("dp", "ctx", None),
        P("dp", "ctx", None),
        P("dp", "ctx", "head"),
    )
    spread = P("dp", ("ctx", "head"), None)
    return jax.shard_map(
        shards, mesh=mesh, in_specs=placed, out_specs=(spread,) * 4, check_vma=False
    )
```

```python
import functools

import jax
import jax.numpy as jnp
from jax import lax
from jax.experimental import pallas as pl
from jax.experimental.pallas import tpu as pltpu
from jax.sharding import PartitionSpec as P

BLOCK = 16
LANES = 128
SUB = 8
UNROLL = 8
FIRST_TILES = 5
EARLY = (0, 2, 3)
VMEM_LIMIT = 20 * 1024 * 1024


def affine(earlier, subsequent):
    return (earlier[0] * subsequent[0], subsequent[0] * earlier[1] + subsequent[1])


def prefix(array, axis, identity, reverse):
    size, position = (lax.axis_size(axis), lax.axis_index(axis))
    everything = jax.tree.map(lambda part: lax.all_gather(part, axis), array)
    start = jax.tree.map(
        lambda part, zero: jnp.broadcast_to(jnp.asarray(zero, part.dtype), part.shape),
        array,
        identity,
    )

    def hop(k, before):
        at = size - 1 - k if reverse else k
        reached = at > position if reverse else at < position
        new = affine(before, jax.tree.map(lambda part: part[at], everything))
        return jax.tree.map(lambda a, b: jnp.where(reached, a, b), new, before)

    return lax.fori_loop(0, size, hop, start)


def group_summary(inputs, step_rate, key_rows, query_rows, grad_out):
    tokens, channels = inputs.shape[1:]
    state_dim = key_rows.shape[2]
    num_blocks = tokens // BLOCK

    def to_blocks(array_in):
        return array_in[0].astype(jnp.float32).reshape(num_blocks, BLOCK, array_in.shape[2])

    def summarize(carried, block_in):
        x, rate, key_blk, query_blk, grad_blk = block_in
        keys_sq = key_blk * key_blk
        step = rate / (1.0 + rate * jnp.sum(keys_sq, axis=1)[:, None])
        decays = 1.0 - step[:, None, :] * keys_sq[:, :, None]
        drives = (step * x)[:, None, :] * key_blk[:, :, None]
        before = jnp.cumprod(decays, axis=0)
        suffix = jnp.cumprod(decays[::-1], axis=0)[::-1]
        after = jnp.concatenate([suffix[1:], jnp.ones_like(decays[:1])], axis=0)
        total = before[-1]
        end = jnp.sum(drives * after, axis=0)
        back = jnp.sum(grad_blk[:, None, :] * query_blk[:, :, None] * before, axis=0)
        return (
            carried[0] * total,
            total * carried[1] + end,
            carried[2] + carried[0] * back,
        ), None

    zero = jnp.zeros((state_dim, channels), jnp.float32)
    blocked = tuple(map(to_blocks, (inputs, step_rate, key_rows, query_rows, grad_out)))
    return lax.scan(summarize, (jnp.ones_like(zero), zero, zero), blocked)[0]


def spread_columns(matrix, table_ref):
    rows, tokens = matrix.shape
    for t in range(tokens):
        table_ref[t] = jnp.broadcast_to(matrix[:, t : t + 1], (rows, LANES))


def halves(value):
    return [value[at : at + SUB] for at in range(0, value.shape[0], SUB)]


def row(ref, tile, t):
    return ref[tile, pl.ds(t, SUB, stride=0), :]


def tile_at(j):
    return pl.ds(j * LANES, LANES)


def lane_sums(values):
    high = values.astype(jnp.bfloat16)
    low = (values - high.astype(jnp.float32)).astype(jnp.bfloat16)
    both = jnp.concatenate([high, low], axis=1)
    ones = jnp.ones((2 * LANES, LANES), jnp.bfloat16)
    return jnp.dot(both, ones, preferred_element_type=jnp.float32)


def first_kernel(offset, width, backwards, has_entry, has_tables, *refs):
    refs = list(refs)
    x_ref, rate_ref, key_ref, query_ref, go_ref = refs[:5]
    del refs[:5]
    entry_ref = refs.pop(0) if has_entry else None
    given = [refs.pop(0), refs.pop(0)] if has_tables else None
    path_ref, end_ref, step_ref, drive_ref, x32_ref, go32_ref, inverse_ref = refs[:7]
    keys_ref, queries_ref = given or refs[7:9]
    states, tokens = key_ref.shape[1:]
    tiles = width // LANES
    fetched = []
    if not has_tables:
        sources = (key_ref, query_ref, rate_ref, x_ref, go_ref)
        kept, semaphores = refs[10:15], refs[15]
        for i, (source, to) in enumerate(zip(sources, kept)):
            if i >= 2:
                source = source.at[:, :, pl.ds(offset, width)]
            fetched.append(pltpu.make_async_copy(source, to, semaphores.at[i]))
            fetched[-1].start()
        key_ref, query_ref, rate_ref, x_ref, go_ref = kept
        fetched[0].wait()
        fetched[1].wait()
    key = key_ref[0].astype(jnp.float32)
    if not has_tables:
        refs[9][...] = key
        spread_columns(key, keys_ref)
        spread_columns(query_ref[0].astype(jnp.float32), queries_ref)
    key_norm = jnp.sum(key * key, axis=0, keepdims=True)
    norm = jnp.transpose(jnp.broadcast_to(key_norm, (LANES, tokens)))
    for copy in fetched[2:]:
        copy.wait()
    for j in range(tiles):
        at = pl.ds((offset if has_tables else 0) + j * LANES, LANES)
        rate = rate_ref[0, :, at]
        x = x_ref[0, :, at].astype(jnp.float32)
        inverse = 1.0 / (1.0 + rate * norm)
        step = rate * inverse
        inverse_ref[j, :tokens] = inverse
        step_ref[j, :tokens] = step
        x32_ref[j, :tokens] = x
        drive_ref[j, :tokens] = step * x
        go32_ref[j, :tokens] = go_ref[0, :, at].astype(jnp.float32)

    if has_entry:
        entry = [halves(entry_ref[:, tile_at(j)]) for j in range(tiles)]
    else:
        entry = [[jnp.zeros((SUB, LANES), jnp.float32)] * (states // SUB)] * tiles

    def finish(state):
        for j in range(tiles):
            end_ref[:, tile_at(j)] = jnp.concatenate(state[j], axis=0)

    def run_states():
        def block(b, state):
            base = b * UNROLL
            state = [list(part) for part in state]
            for u in range(UNROLL):
                k = halves(keys_ref[base + u])
                k2 = [part * part for part in k]
                for j in range(tiles):
                    step = row(step_ref, j, base + u)
                    drive = row(drive_ref, j, base + u)
                    for h in range(len(k)):
                        state[j][h] = (1.0 - step * k2[h]) * state[j][h] + drive * k[h]
                        path_ref[base + u, pl.ds(h * SUB, SUB), tile_at(j)] = state[j][h]
            return state

        finish(lax.fori_loop(0, tokens // UNROLL, block, entry))

    def run_grads():
        def block(i, state):
            base = tokens - UNROLL - i * UNROLL
            state = [list(part) for part in state]
            for u in reversed(range(UNROLL)):
                k2 = [part * part for part in halves(keys_ref[base + u])]
                q = halves(queries_ref[base + u])
                for j in range(tiles):
                    step = row(step_ref, j, base + u)
                    go = row(go32_ref, j, base + u)
                    for h in range(len(q)):
                        grad = go * q[h] + state[j][h]
                        path_ref[base + u, pl.ds(h * SUB, SUB), tile_at(j)] = grad
                        state[j][h] = (1.0 - step * k2[h]) * grad
            return state

        finish(lax.fori_loop(0, tokens // UNROLL, block, entry))

    choose(backwards, run_grads, run_states)


def choose(flag, if_set, if_not):
    if flag is None:
        group = lax.axis_index("ctx")
        pl.when(group != 0)(if_set)
        pl.when(group == 0)(if_not)
    else:
        (if_set if flag else if_not)()


def second_kernel(onwards_here, last, heads, has_start, *refs):
    refs = list(refs)
    entry_ref, path_ref, step_ref, drive_ref, x32_ref, go32_ref, inverse_ref = refs[:7]
    keys_ref, queries_ref = refs[7:9]
    del refs[:9]
    start_ref = refs.pop(0) if has_start else None
    before = [refs.pop(0) for _ in range(4)] if last else None
    key_ref = refs.pop(0) if last else None
    if not last:
        del refs[0]
    piece_refs = refs[:heads]
    passed = [refs.pop(heads), refs.pop(heads)] if last else None
    key_part_ref, query_part_ref, norm_ref, dot_ref, weighted_ref = refs[heads : heads + 5]
    tokens, states = keys_ref.shape[:2]
    tiles = step_ref.shape[0]
    pair = range(states // SUB)

    def path_at(t, h, j):
        return path_ref[t, pl.ds(h * SUB, SUB), tile_at(j)]

    def step_through(back):
        order = list(reversed(range(UNROLL))) if back else list(range(UNROLL))
        work = [(u, j) for u in order for j in range(tiles)]

        def block(i, state):
            base = tokens - UNROLL - i * UNROLL if back else i * UNROLL
            state = [list(part) for part in state]
            if back:
                top = base + UNROLL - 1
                held = [[path_at(top, h, j) for h in pair] for j in range(tiles)]

            def load(u, j):
                rows = [row(ref, j, base + u) for ref in (step_ref, drive_ref, go32_ref)]
                if not back:
                    return rows, [path_at(base + u, h, j) for h in pair]
                earlier = [path_at(jnp.maximum(base + u - 1, 0), h, j) for h in pair]
                if u == 0:
                    for h in pair:
                        start = start_ref[pl.ds(h * SUB, SUB), tile_at(j)] if has_start else 0.0
                        earlier[h] = jnp.where(base == 0, start, earlier[h])
                return rows, earlier

            ahead = load(*work[0])
            for at, (u, j) in enumerate(work):
                t = base + u
                (step, drive, go), loaded = ahead
                if j == 0:
                    k, q = halves(keys_ref[t]), halves(queries_ref[t])
                    k2 = [part * part for part in k]
                if at + 1 < len(work):
                    ahead = load(*work[at + 1])
                dots, weights, terms = [], [], []
                for h in pair:
                    decay = 1.0 - step * k2[h]
                    if back:
                        grad = go * q[h] + state[j][h]
                        here, previous = held[j][h], loaded[h]
                        held[j][h] = previous
                        state[j][h] = decay * grad
                    else:
                        grad, previous = loaded[h], state[j][h]
                        here = decay * previous + drive * k[h]
                        state[j][h] = here
                    weight = grad * previous
                    dots.append(grad * k[h])
                    weights.append(weight * k2[h])
                    terms += [grad * drive, weight * step, here * go]
                rows = pl.ds(pl.multiple_of(t * SUB, SUB), SUB)
                dot_ref[j, rows, :] = sum(dots[1:], dots[0])
                weighted_ref[j, rows, :] = sum(weights[1:], weights[0])
                sums = terms if j == 0 else [a + b for a, b in zip(sums, terms)]
                if j < tiles - 1:
                    continue
                for h in pair:
                    by_drive, by_decay, by_query = sums[3 * h : 3 * h + 3]
                    rows = pl.ds(pl.multiple_of(t * states + h * SUB, SUB), SUB)
                    by_key = by_drive - (2.0 * k[h]) * by_decay
                    if last:
                        by_key = by_key + before[0][rows, :]
                        by_query = by_query + before[1][rows, :]
                    key_part_ref[rows, :] = by_key
                    query_part_ref[rows, :] = by_query
            return state

        entry = [halves(entry_ref[:, tile_at(j)]) for j in range(tiles)]
        lax.fori_loop(0, tokens // UNROLL, block, entry)

    choose(onwards_here, lambda: step_through(False), lambda: step_through(True))

    part = tokens // heads
    rows = 2 * SUB
    position = lax.axis_index("head")
    width = tiles * LANES
    if last:
        half = before[3].shape[1] // 2
        for i, to in enumerate(passed):
            to[...] = before[3][:, pl.ds(i * half, half)]
    for d in range(heads):
        for r in range(part // rows):
            base = pl.multiple_of((position ^ d) * part + r * rows, rows)
            norm_sum = before[2][pl.ds(base, rows), :] if last else None
            for j in range(tiles):
                dot, weighted = (
                    sum(ref[j, pl.ds(base * SUB + s, rows, stride=SUB), :] for s in range(SUB))
                    for ref in (dot_ref, weighted_ref)
                )
                step, x, inverse = (
                    ref[j, pl.ds(base, rows), :] for ref in (step_ref, x32_ref, inverse_ref)
                )
                grad_step = x * dot - weighted
                grad_rate = grad_step * inverse * inverse
                to = pl.ds(r * rows, rows)
                piece_refs[d][to, tile_at(j)] = (step * dot).astype(jnp.bfloat16)
                piece_refs[d][to, tile_at(tiles + j)] = grad_rate.astype(jnp.bfloat16)
                term = grad_step * step * step
                norm_sum = term if norm_sum is None else norm_sum + term
            norm_ref[pl.ds(base, rows), :] = norm_sum
    if not last:
        return

    key = key_ref[...]
    norm_row = jnp.sum(jnp.transpose(norm_ref[...]), axis=0, keepdims=True)
    lane = lax.broadcasted_iota(jnp.int32, (states, tokens), 1)
    totals = []
    for ref in (key_part_ref, query_part_ref):
        total = jnp.zeros((states, tokens), jnp.float32)
        for base in range(0, tokens, tokens // 2):
            sums = lane_sums(ref[pl.ds(base * states, tokens // 2 * states), :])
            for t in range(tokens // 2):
                total = jnp.where(lane == base + t, sums[t * states : (t + 1) * states], total)
        totals.append(total)
    sums_ref = refs[heads + 5]
    sums_ref[:states] = totals[0] - 2.0 * key * norm_row
    sums_ref[states:] = totals[1]
    quarters = 2 * states // SUB
    lane = lax.broadcasted_iota(jnp.int32, (SUB, tokens), 1) // part
    for d in range(heads):
        shift = (heads - (position ^ d)) * part
        packed = None
        for i in range(quarters):
            turned = pltpu.roll(
                sums_ref[SUB * i : SUB * i + SUB], lax.rem(shift + i * part, tokens), 1
            )
            packed = turned if packed is None else jnp.where(lane == i, turned, packed)
        high = packed.astype(jnp.bfloat16).astype(jnp.float32)
        both = jnp.concatenate([high, packed - high], axis=0).astype(jnp.bfloat16)
        tail = pl.ds(2 * width, LANES)
        piece_refs[d][:rows, tail] = both
        piece_refs[d][rows:, tail] = jnp.zeros((part - rows, LANES), jnp.bfloat16)


def place(out_ref, piece, at, d, offset, width, channels, semaphore):
    to = pl.multiple_of((lax.axis_index("head") ^ d) * channels + offset, LANES)
    copy = pltpu.make_async_copy(
        piece.at[:, pl.ds(at, width)], out_ref.at[0, :, pl.ds(to, width)], semaphore
    )
    copy.start()
    return copy


def early_kernel(channels, distances, *refs):
    *pieces, own, in_ref, rate_ref, semaphores = refs
    first = pieces[0].shape[1] // 2
    width = channels - first
    copies = []
    for i, out in enumerate((in_ref, rate_ref)):
        copies.append(
            place(out, own, i * width, 0, first, width, channels, semaphores.at[len(pieces), i])
        )
        for p, d in enumerate(distances):
            copies.append(
                place(out, pieces[p], i * first, d, 0, first, channels, semaphores.at[p, i])
            )
    for copy in copies:
        copy.wait()


def late_kernel(heads, channels, *refs):
    pieces, passed = refs[:heads][::-1], refs[heads : heads + 2]
    *out_refs, key_ref, query_ref, key_kept, query_kept, semaphores = refs[heads + 4 :]
    states, part = key_ref.shape[1:]
    width = (pieces[0].shape[1] - LANES) // 2
    copies = []
    for d in range(1, heads):
        for i, out in enumerate(out_refs):
            copies.append(
                place(
                    out, pieces[d], i * width, d, channels - width, width, channels,
                    semaphores.at[d, i],
                )
            )
    for i, out in enumerate(out_refs):
        copies.append(
            place(out, passed[i], 0, 1, 0, channels - width, channels, semaphores.at[heads, i])
        )
    total = None
    for d in range(heads):
        tail = pl.ds(2 * width, LANES)
        both = pieces[d][: 2 * SUB, tail].astype(jnp.float32)
        both = both[:SUB] + both[SUB:]
        total = both if total is None else total + both
    for i in range(states // SUB):
        key_kept[0, SUB * i : SUB * i + SUB] = total[:, i * part : (i + 1) * part]
        at = states // SUB + i
        query_kept[0, SUB * i : SUB * i + SUB] = total[:, at * part : (at + 1) * part]
    for i, (kept, out) in enumerate(((key_kept, key_ref), (query_kept, query_ref))):
        copies.append(pltpu.make_async_copy(kept, out, semaphores.at[0, i]))
        copies[-1].start()
    for copy in copies:
        copy.wait()


def shards(inputs, step_rate, key_rows, query_rows, grad_out):
    _, tokens, channels = inputs.shape
    states = key_rows.shape[2]
    heads = lax.axis_size("head")
    groups = lax.axis_size("ctx")
    part = tokens // heads
    tiles = channels // LANES
    first_width = tiles * FIRST_TILES // 8 * LANES
    widths = (first_width, channels - first_width)
    key_cols = jnp.swapaxes(key_rows, 1, 2)
    query_cols = jnp.swapaxes(query_rows, 1, 2)
    f32 = jnp.float32
    bf16 = jnp.bfloat16
    params = pltpu.CompilerParams(vmem_limit_bytes=VMEM_LIMIT)
    whole = pl.BlockSpec(memory_space=pltpu.VMEM)
    anywhere = pl.BlockSpec(memory_space=pl.ANY)
    table = pltpu.VMEM((tokens, states, LANES), f32)

    def cost(width, passes):
        elements = tokens * states * width
        return pl.CostEstimate(
            flops=passes * elements, bytes_accessed=4 * elements, transcendentals=0
        )

    def first(c, backwards, tables=(), entry=None):
        width = widths[c]
        arrays = [inputs, step_rate, key_cols, query_cols, grad_out]
        specs, scratch = [whole] * 5, []
        if c == 0:
            specs = [anywhere] * 5
            arrays = [pltpu.with_memory_space_constraint(a, pltpu.HBM) for a in arrays]
            scratch = [pltpu.VMEM((1, states, tokens), bf16)] * 2
            scratch += [pltpu.VMEM((1, tokens, width), a.dtype) for a in (step_rate, inputs, grad_out)]
            scratch += [pltpu.SemaphoreType.DMA((5,))]
        extra = [*(() if entry is None else (entry,)), *tables[:2]]
        out_shape = [
            pltpu.VMEM((tokens, states, width), f32),
            jax.ShapeDtypeStruct((states, width), f32),
        ]
        out_shape += [pltpu.VMEM((width // LANES, tokens + SUB, LANES), f32)] * 5
        if not tables:
            out_shape += [table] * 2 + [pltpu.VMEM((states, tokens), f32)]
        path, end, *carried = pl.pallas_call(
            functools.partial(
                first_kernel, sum(widths[:c]), width, backwards, entry is not None, bool(tables)
            ),
            in_specs=specs + [whole] * len(extra),
            out_specs=[whole] * len(out_shape),
            out_shape=out_shape,
            scratch_shapes=scratch,
            compiler_params=params,
            cost_estimate=cost(width, 5),
        )(*arrays, *extra)
        return path, end, carried[:5], tuple(tables) or tuple(carried[5:])

    def second(c, onwards_here, entry, carried, tables, start, before):
        width = widths[c]
        last = c == 1
        keys, queries, key = tables
        extra = [*(() if start is None else (start,)), *before, *((key,) if last else ())]
        specs = [whole] * (9 + len(extra))
        if not last:
            extra, specs = extra + [work[1][1][0]], specs + [anywhere]
        parts = pltpu.VMEM((width // LANES, (tokens + 1) * SUB, LANES), f32)
        sums = pltpu.VMEM(((tokens + 1) * states, LANES), f32)
        pieces = [jax.ShapeDtypeStruct((part, 2 * width + LANES * last), bf16)] * heads
        if last:
            pieces += [jax.ShapeDtypeStruct((part, channels - width), bf16)] * 2
        results = pl.pallas_call(
            functools.partial(second_kernel, onwards_here, last, heads, start is not None),
            in_specs=specs,
            out_specs=[whole] * (len(pieces) + 3),
            out_shape=pieces + [sums, sums, pltpu.VMEM((tokens, LANES), f32)],
            scratch_shapes=[parts, parts] + [pltpu.VMEM((2 * states, tokens), f32)] * last,
            compiler_params=params,
            cost_estimate=cost(width, 20),
        )(entry, *carried, keys, queries, *extra)
        return results[:-3], results[-3:]

    entries = starts = here = None
    if groups != 2:
        here = False
        product, end, back = group_summary(inputs, step_rate, key_rows, query_rows, grad_out)
        unit = (jnp.ones_like(product), jnp.zeros_like(product))
        starts = prefix((product, end), "ctx", unit, False)[1]
        entries = prefix((product, back), "ctx", unit, True)[1]

    def part_of(array, c):
        return None if array is None else array[:, sum(widths[:c]) : sum(widths[: c + 1])]

    def send(piece, d):
        return lax.ppermute(piece, "head", [(s, s ^ d) for s in range(heads)])

    tables, work = (), []
    for c in range(2):
        path, end, carried, tables = first(c, here, tables, part_of(starts, c))
        entry = part_of(entries, c)
        if entry is None:
            entry = lax.ppermute(end, "ctx", [(0, 1), (1, 0)])
        work.append((entry, [path, *carried], part_of(starts, c)))

    def call_second(c, before):
        entry, carried, start = work[c]
        return second(c, here, entry, carried, tables, start, before)

    away = list(range(heads - 1, 0, -1))
    pieces, before = call_second(0, ())
    arrived = {d: send(pieces[d], d) for d in away if d != 1}
    arrived[0] = pieces[0]
    *pieces, near_in, near_rate = call_second(1, (*before, pieces[1]))[0]
    late = [*(send(pieces[d], d) for d in away), pieces[0], send(near_in, 1), send(near_rate, 1)]

    out = [jax.ShapeDtypeStruct((1, part, heads * channels), bf16)] * 2
    outs = pl.pallas_call(
        functools.partial(early_kernel, channels, EARLY),
        in_specs=[whole] * heads,
        out_specs=[anywhere] * 2,
        out_shape=out,
        scratch_shapes=[pltpu.SemaphoreType.DMA((heads, 2))],
        compiler_params=params,
    )(*[arrived[d] for d in EARLY], pieces[0])
    small = (1, states, part)
    grad_in, grad_rate, grad_key, grad_query = pl.pallas_call(
        functools.partial(late_kernel, heads, channels),
        in_specs=[whole] * (heads + 2) + [anywhere] * 2,
        out_specs=[anywhere] * 4,
        out_shape=out + [jax.ShapeDtypeStruct(small, f32)] * 2,
        scratch_shapes=[pltpu.VMEM(small, f32)] * 2 + [pltpu.SemaphoreType.DMA((heads + 1, 2))],
        input_output_aliases={heads + 2: 0, heads + 3: 1},
        compiler_params=params,
    )(*late, *outs)
    return (grad_in, grad_rate, jnp.swapaxes(grad_key, 1, 2), jnp.swapaxes(grad_query, 1, 2))


def solution(mesh):
    placed = (
        P("dp", "ctx", "head"),
        P("dp", "ctx", "head"),
        P("dp", "ctx", None),
        P("dp", "ctx", None),
        P("dp", "ctx", "head"),
    )
    spread = P("dp", ("ctx", "head"), None)
    return jax.shard_map(
        shards, mesh=mesh, in_specs=placed, out_specs=(spread,) * 4, check_vma=False
    )
```

```python
import functools

import jax
import jax.numpy as jnp
from jax import lax
from jax.experimental import pallas as pl
from jax.experimental.pallas import tpu as pltpu
from jax.sharding import PartitionSpec as P

BLOCK = 16
LANES = 128
SUB = 8
UNROLL = 8
FIRST_TILES = 5
EARLY = (0, 2, 3, 1)
VMEM_LIMIT = 20 * 1024 * 1024


def affine(earlier, subsequent):
    return (earlier[0] * subsequent[0], subsequent[0] * earlier[1] + subsequent[1])


def prefix(array, axis, identity, reverse):
    size, position = (lax.axis_size(axis), lax.axis_index(axis))
    everything = jax.tree.map(lambda part: lax.all_gather(part, axis), array)
    start = jax.tree.map(
        lambda part, zero: jnp.broadcast_to(jnp.asarray(zero, part.dtype), part.shape),
        array,
        identity,
    )

    def hop(k, before):
        at = size - 1 - k if reverse else k
        reached = at > position if reverse else at < position
        new = affine(before, jax.tree.map(lambda part: part[at], everything))
        return jax.tree.map(lambda a, b: jnp.where(reached, a, b), new, before)

    return lax.fori_loop(0, size, hop, start)


def group_summary(inputs, step_rate, key_rows, query_rows, grad_out):
    tokens, channels = inputs.shape[1:]
    state_dim = key_rows.shape[2]
    num_blocks = tokens // BLOCK

    def to_blocks(array_in):
        return array_in[0].astype(jnp.float32).reshape(num_blocks, BLOCK, array_in.shape[2])

    def summarize(carried, block_in):
        x, rate, key_blk, query_blk, grad_blk = block_in
        keys_sq = key_blk * key_blk
        step = rate / (1.0 + rate * jnp.sum(keys_sq, axis=1)[:, None])
        decays = 1.0 - step[:, None, :] * keys_sq[:, :, None]
        drives = (step * x)[:, None, :] * key_blk[:, :, None]
        before = jnp.cumprod(decays, axis=0)
        suffix = jnp.cumprod(decays[::-1], axis=0)[::-1]
        after = jnp.concatenate([suffix[1:], jnp.ones_like(decays[:1])], axis=0)
        total = before[-1]
        end = jnp.sum(drives * after, axis=0)
        back = jnp.sum(grad_blk[:, None, :] * query_blk[:, :, None] * before, axis=0)
        return (
            carried[0] * total,
            total * carried[1] + end,
            carried[2] + carried[0] * back,
        ), None

    zero = jnp.zeros((state_dim, channels), jnp.float32)
    blocked = tuple(map(to_blocks, (inputs, step_rate, key_rows, query_rows, grad_out)))
    return lax.scan(summarize, (jnp.ones_like(zero), zero, zero), blocked)[0]


def spread_columns(matrix, table_ref):
    rows, tokens = matrix.shape
    for t in range(tokens):
        table_ref[t] = jnp.broadcast_to(matrix[:, t : t + 1], (rows, LANES))


def halves(value):
    return [value[at : at + SUB] for at in range(0, value.shape[0], SUB)]


def row(ref, tile, t):
    return ref[tile, pl.ds(t, SUB, stride=0), :]


def norm_row(ref, t):
    return ref[pl.ds(t, SUB, stride=0), :]


def tile_at(j):
    return pl.ds(j * LANES, LANES)


def lane_sums(values):
    high = values.astype(jnp.bfloat16)
    low = (values - high.astype(jnp.float32)).astype(jnp.bfloat16)
    both = jnp.concatenate([high, low], axis=1)
    ones = jnp.ones((2 * LANES, LANES), jnp.bfloat16)
    return jnp.dot(both, ones, preferred_element_type=jnp.float32)


def first_kernel(offset, width, backwards, has_entry, has_tables, *refs):
    refs = list(refs)
    x_ref, rate_ref, key_ref, query_ref, go_ref = refs[:5]
    del refs[:5]
    entry_ref = refs.pop(0) if has_entry else None
    given = [refs.pop(0), refs.pop(0)] if has_tables else None
    path_ref, end_ref, step_ref, drive_ref, x32_ref, go32_ref, inverse_ref = refs[:7]
    keys_ref, queries_ref = given or refs[7:9]
    states, tokens = key_ref.shape[1:]
    tiles = width // LANES
    fetched = []
    if not has_tables:
        sources = (key_ref, query_ref, rate_ref, x_ref, go_ref)
        kept, semaphores = refs[9:14], refs[14]
        for i, (source, to) in enumerate(zip(sources, kept)):
            if i >= 2:
                source = source.at[:, :, pl.ds(offset, width)]
            fetched.append(pltpu.make_async_copy(source, to, semaphores.at[i]))
            fetched[-1].start()
        key_ref, query_ref, rate_ref, x_ref, go_ref = kept
        fetched[0].wait()
        fetched[1].wait()
    key = key_ref[0].astype(jnp.float32)
    if not has_tables:
        spread_columns(key, keys_ref)
        spread_columns(query_ref[0].astype(jnp.float32), queries_ref)
    key_norm = jnp.sum(key * key, axis=0, keepdims=True)
    norm = jnp.transpose(jnp.broadcast_to(key_norm, (LANES, tokens)))
    for copy in fetched[2:]:
        copy.wait()
    for j in range(tiles):
        at = pl.ds((offset if has_tables else 0) + j * LANES, LANES)
        rate = rate_ref[0, :, at]
        x = x_ref[0, :, at].astype(jnp.float32)
        inverse = 1.0 / (1.0 + rate * norm)
        step = rate * inverse
        inverse_ref[j, :tokens] = inverse
        step_ref[j, :tokens] = step
        x32_ref[j, :tokens] = x
        drive_ref[j, :tokens] = step * x
        go32_ref[j, :tokens] = go_ref[0, :, at].astype(jnp.float32)

    if has_entry:
        entry = [halves(entry_ref[:, tile_at(j)]) for j in range(tiles)]
    else:
        entry = [[jnp.zeros((SUB, LANES), jnp.float32)] * (states // SUB)] * tiles

    def finish(state):
        for j in range(tiles):
            end_ref[:, tile_at(j)] = jnp.concatenate(state[j], axis=0)

    def run_states():
        def block(b, state):
            base = b * UNROLL
            state = [list(part) for part in state]
            for u in range(UNROLL):
                k = halves(keys_ref[base + u])
                k2 = [part * part for part in k]
                for j in range(tiles):
                    step = row(step_ref, j, base + u)
                    drive = row(drive_ref, j, base + u)
                    for h in range(len(k)):
                        state[j][h] = (1.0 - step * k2[h]) * state[j][h] + drive * k[h]
                        path_ref[base + u, pl.ds(h * SUB, SUB), tile_at(j)] = state[j][h]
            return state

        finish(lax.fori_loop(0, tokens // UNROLL, block, entry))

    def run_grads():
        def block(i, state):
            base = tokens - UNROLL - i * UNROLL
            state = [list(part) for part in state]
            for u in reversed(range(UNROLL)):
                k2 = [part * part for part in halves(keys_ref[base + u])]
                q = halves(queries_ref[base + u])
                for j in range(tiles):
                    step = row(step_ref, j, base + u)
                    go = row(go32_ref, j, base + u)
                    for h in range(len(q)):
                        grad = go * q[h] + state[j][h]
                        path_ref[base + u, pl.ds(h * SUB, SUB), tile_at(j)] = grad
                        state[j][h] = (1.0 - step * k2[h]) * grad
            return state

        finish(lax.fori_loop(0, tokens // UNROLL, block, entry))

    choose(backwards, run_grads, run_states)


def choose(flag, if_set, if_not):
    if flag is None:
        group = lax.axis_index("ctx")
        pl.when(group != 0)(if_set)
        pl.when(group == 0)(if_not)
    else:
        (if_set if flag else if_not)()


def second_kernel(onwards_here, last, heads, has_start, *refs):
    refs = list(refs)
    entry_ref, path_ref, step_ref, drive_ref, x32_ref, go32_ref, inverse_ref = refs[:7]
    keys_ref, queries_ref = refs[7:9]
    del refs[:9]
    start_ref = refs.pop(0) if has_start else None
    before = [refs.pop(0) for _ in range(3)] if last else None
    if not last:
        del refs[0]
    piece_refs = refs[:heads]
    key_part_ref, query_part_ref, norm_ref, dot_ref, weighted_ref = refs[heads : heads + 5]
    tokens, states = keys_ref.shape[:2]
    tiles = step_ref.shape[0]
    pair = range(states // SUB)

    def path_at(t, h, j):
        return path_ref[t, pl.ds(h * SUB, SUB), tile_at(j)]

    def step_through(back):
        order = list(reversed(range(UNROLL))) if back else list(range(UNROLL))
        work = [(u, j) for u in order for j in range(tiles)]

        def block(i, state):
            base = tokens - UNROLL - i * UNROLL if back else i * UNROLL
            state = [list(part) for part in state]
            if back:
                top = base + UNROLL - 1
                held = [[path_at(top, h, j) for h in pair] for j in range(tiles)]

            def load(u, j):
                rows = [row(ref, j, base + u) for ref in (step_ref, drive_ref, go32_ref)]
                if not back:
                    return rows, [path_at(base + u, h, j) for h in pair]
                earlier = [path_at(jnp.maximum(base + u - 1, 0), h, j) for h in pair]
                if u == 0:
                    for h in pair:
                        start = start_ref[pl.ds(h * SUB, SUB), tile_at(j)] if has_start else 0.0
                        earlier[h] = jnp.where(base == 0, start, earlier[h])
                return rows, earlier

            ahead = load(*work[0])
            for at, (u, j) in enumerate(work):
                t = base + u
                (step, drive, go), loaded = ahead
                if j == 0:
                    k, q = halves(keys_ref[t]), halves(queries_ref[t])
                    k2 = [part * part for part in k]
                if at + 1 < len(work):
                    ahead = load(*work[at + 1])
                dots, weights, terms = [], [], []
                for h in pair:
                    decay = 1.0 - step * k2[h]
                    if back:
                        grad = go * q[h] + state[j][h]
                        here, previous = held[j][h], loaded[h]
                        held[j][h] = previous
                        state[j][h] = decay * grad
                    else:
                        grad, previous = loaded[h], state[j][h]
                        here = decay * previous + drive * k[h]
                        state[j][h] = here
                    weight = grad * previous
                    dots.append(grad * k[h])
                    weights.append(weight * k2[h])
                    terms += [grad * drive, weight * step, here * go]
                rows = pl.ds(pl.multiple_of(t * SUB, SUB), SUB)
                dot_ref[j, rows, :] = sum(dots[1:], dots[0])
                weighted_ref[j, rows, :] = sum(weights[1:], weights[0])
                sums = terms if j == 0 else [a + b for a, b in zip(sums, terms)]
                if j < tiles - 1:
                    continue
                for h in pair:
                    by_drive, by_decay, by_query = sums[3 * h : 3 * h + 3]
                    rows = pl.ds(pl.multiple_of(t * states + h * SUB, SUB), SUB)
                    by_key = by_drive - (2.0 * k[h]) * by_decay
                    if last:
                        by_key = by_key + before[0][rows, :]
                        by_query = by_query + before[1][rows, :]
                    key_part_ref[rows, :] = by_key
                    query_part_ref[rows, :] = by_query
            return state

        entry = [halves(entry_ref[:, tile_at(j)]) for j in range(tiles)]
        lax.fori_loop(0, tokens // UNROLL, block, entry)

    choose(onwards_here, lambda: step_through(False), lambda: step_through(True))

    part = tokens // heads
    rows = 2 * SUB
    position = lax.axis_index("head")
    width = tiles * LANES
    for d in range(heads):
        for r in range(part // rows):
            base = pl.multiple_of((position ^ d) * part + r * rows, rows)
            norm_sum = before[2][pl.ds(base, rows), :] if last else None
            for j in range(tiles):
                dot, weighted = (
                    sum(ref[j, pl.ds(base * SUB + s, rows, stride=SUB), :] for s in range(SUB))
                    for ref in (dot_ref, weighted_ref)
                )
                step, x, inverse = (
                    ref[j, pl.ds(base, rows), :] for ref in (step_ref, x32_ref, inverse_ref)
                )
                grad_step = x * dot - weighted
                grad_rate = grad_step * inverse * inverse
                to = j * LANES
                piece_refs[d][pl.ds(r * rows, rows), pl.ds(to, LANES)] = (step * dot).astype(
                    jnp.bfloat16
                )
                to += width
                piece_refs[d][pl.ds(r * rows, rows), pl.ds(to, LANES)] = grad_rate.astype(
                    jnp.bfloat16
                )
                term = grad_step * step * step
                norm_sum = term if norm_sum is None else norm_sum + term
            norm_ref[pl.ds(base, rows), :] = norm_sum
    if not last:
        return

    tails_ref = refs[heads + 5]
    lane = lax.broadcasted_iota(jnp.int32, (SUB, LANES), 1)
    for h in range(heads):
        packed = jnp.zeros((SUB, LANES), jnp.float32)
        for i, ref in enumerate((key_part_ref, query_part_ref)):
            here = range(h * part, (h + 1) * part)
            values = ref[pl.ds(h * part * states, part * states), :]
            if i == 0:
                norms = [
                    2.0 * keys_ref[t] * jnp.concatenate([norm_row(norm_ref, t)] * len(pair), axis=0)
                    for t in here
                ]
                values = values - jnp.concatenate(norms, axis=0)
            sums = lane_sums(values)
            for t in range(part):
                for half in pair:
                    at = t * states + half * SUB
                    to = (i * len(pair) + half) * part + t
                    packed = jnp.where(lane == to, sums[at : at + SUB], packed)
        tails_ref[h] = packed
    for d in range(heads):
        packed = tails_ref[position ^ d]
        high = packed.astype(jnp.bfloat16).astype(jnp.float32)
        both = jnp.concatenate([high, packed - high], axis=0).astype(jnp.bfloat16)
        tail = pl.ds(2 * width, LANES)
        piece_refs[d][:rows, tail] = both
        piece_refs[d][rows:, tail] = jnp.zeros((part - rows, LANES), jnp.bfloat16)


def place(out_refs, piece, d, offset, width, channels, semaphores):
    at = pl.multiple_of((lax.axis_index("head") ^ d) * channels + offset, LANES)
    copies = []
    for i, out in enumerate(out_refs):
        copies.append(
            pltpu.make_async_copy(
                piece.at[:, pl.ds(i * width, width)],
                out.at[0, :, pl.ds(at, width)],
                semaphores.at[i],
            )
        )
        copies[-1].start()
    return copies


def early_kernel(channels, distances, *refs):
    *pieces, own, in_ref, rate_ref, semaphores = refs
    out_refs = (in_ref, rate_ref)
    first = pieces[0].shape[1] // 2
    width = channels - first
    copies = place(out_refs, own, 0, first, width, channels, semaphores.at[len(pieces)])
    for i, d in enumerate(distances):
        copies += place(out_refs, pieces[i], d, 0, first, channels, semaphores.at[i])
    for copy in copies:
        copy.wait()


def late_kernel(heads, channels, *refs):
    pieces = refs[:heads][::-1]
    *out_refs, key_ref, query_ref, key_kept, query_kept, semaphores = refs[heads + 2 :]
    states, part = key_ref.shape[1:]
    width = (pieces[0].shape[1] - LANES) // 2
    copies = []
    for d in range(1, heads):
        copies += place(
            out_refs, pieces[d], d, channels - width, width, channels, semaphores.at[d]
        )
    total = None
    for d in range(heads):
        tail = pl.ds(2 * width, LANES)
        both = pieces[d][: 2 * SUB, tail].astype(jnp.float32)
        both = both[:SUB] + both[SUB:]
        total = both if total is None else total + both
    for i in range(states // SUB):
        key_kept[0, SUB * i : SUB * i + SUB] = total[:, i * part : (i + 1) * part]
        at = states // SUB + i
        query_kept[0, SUB * i : SUB * i + SUB] = total[:, at * part : (at + 1) * part]
    for i, (kept, out) in enumerate(((key_kept, key_ref), (query_kept, query_ref))):
        copies.append(pltpu.make_async_copy(kept, out, semaphores.at[0, i]))
        copies[-1].start()
    for copy in copies:
        copy.wait()


def shards(inputs, step_rate, key_rows, query_rows, grad_out):
    _, tokens, channels = inputs.shape
    states = key_rows.shape[2]
    heads = lax.axis_size("head")
    groups = lax.axis_size("ctx")
    part = tokens // heads
    tiles = channels // LANES
    first_width = tiles * FIRST_TILES // 8 * LANES
    widths = (first_width, channels - first_width)
    key_cols = jnp.swapaxes(key_rows, 1, 2)
    query_cols = jnp.swapaxes(query_rows, 1, 2)
    f32 = jnp.float32
    bf16 = jnp.bfloat16
    params = pltpu.CompilerParams(vmem_limit_bytes=VMEM_LIMIT)
    whole = pl.BlockSpec(memory_space=pltpu.VMEM)
    anywhere = pl.BlockSpec(memory_space=pl.ANY)
    table = pltpu.VMEM((tokens, states, LANES), f32)

    def cost(width, passes):
        elements = tokens * states * width
        return pl.CostEstimate(
            flops=passes * elements, bytes_accessed=4 * elements, transcendentals=0
        )

    def first(c, backwards, tables=(), entry=None):
        width = widths[c]
        arrays = [inputs, step_rate, key_cols, query_cols, grad_out]
        specs, scratch = [whole] * 5, []
        if c == 0:
            specs = [anywhere] * 5
            arrays = [pltpu.with_memory_space_constraint(a, pltpu.HBM) for a in arrays]
            scratch = [pltpu.VMEM((1, states, tokens), bf16)] * 2
            scratch += [pltpu.VMEM((1, tokens, width), a.dtype) for a in (step_rate, inputs, grad_out)]
            scratch += [pltpu.SemaphoreType.DMA((5,))]
        extra = [*(() if entry is None else (entry,)), *tables[:2]]
        out_shape = [
            pltpu.VMEM((tokens, states, width), f32),
            jax.ShapeDtypeStruct((states, width), f32),
        ]
        out_shape += [pltpu.VMEM((width // LANES, tokens + SUB, LANES), f32)] * 5
        if not tables:
            out_shape += [table] * 2
        path, end, *carried = pl.pallas_call(
            functools.partial(
                first_kernel, sum(widths[:c]), width, backwards, entry is not None, bool(tables)
            ),
            in_specs=specs + [whole] * len(extra),
            out_specs=[whole] * len(out_shape),
            out_shape=out_shape,
            scratch_shapes=scratch,
            compiler_params=params,
            cost_estimate=cost(width, 5),
        )(*arrays, *extra)
        return path, end, carried[:5], tuple(tables) or tuple(carried[5:])

    def second(c, onwards_here, entry, carried, tables, start, before):
        width = widths[c]
        last = c == 1
        keys, queries = tables
        extra = [*(() if start is None else (start,)), *before]
        specs = [whole] * (9 + len(extra))
        if not last:
            extra, specs = extra + [work[1][1][0]], specs + [anywhere]
        parts = pltpu.VMEM((width // LANES, (tokens + 1) * SUB, LANES), f32)
        sums = pltpu.VMEM(((tokens + 1) * states, LANES), f32)
        pieces = [jax.ShapeDtypeStruct((part, 2 * width + LANES * last), bf16)] * heads
        results = pl.pallas_call(
            functools.partial(second_kernel, onwards_here, last, heads, start is not None),
            in_specs=specs,
            out_specs=[whole] * (heads + 3),
            out_shape=pieces + [sums, sums, pltpu.VMEM((tokens + SUB, LANES), f32)],
            scratch_shapes=[parts, parts] + [pltpu.VMEM((heads, SUB, LANES), f32)] * last,
            compiler_params=params,
            cost_estimate=cost(width, 20),
        )(entry, *carried, keys, queries, *extra)
        return results[:heads], results[heads:]

    entries = starts = here = None
    if groups != 2:
        here = False
        product, end, back = group_summary(inputs, step_rate, key_rows, query_rows, grad_out)
        unit = (jnp.ones_like(product), jnp.zeros_like(product))
        starts = prefix((product, end), "ctx", unit, False)[1]
        entries = prefix((product, back), "ctx", unit, True)[1]

    def part_of(array, c):
        return None if array is None else array[:, sum(widths[:c]) : sum(widths[: c + 1])]

    def send(piece, d):
        return lax.ppermute(piece, "head", [(s, s ^ d) for s in range(heads)])

    tables, work = (), []
    for c in range(2):
        path, end, carried, tables = first(c, here, tables, part_of(starts, c))
        entry = part_of(entries, c)
        if entry is None:
            entry = lax.ppermute(end, "ctx", [(0, 1), (1, 0)])
        work.append((entry, [path, *carried], part_of(starts, c)))

    def call_second(c, before):
        entry, carried, start = work[c]
        return second(c, here, entry, carried, tables, start, before)

    away = list(range(heads - 1, 0, -1))
    pieces, before = call_second(0, ())
    arrived = {d: send(pieces[d], d) for d in away}
    arrived[0] = pieces[0]
    pieces, _ = call_second(1, before)
    late = [*(send(pieces[d], d) for d in away), pieces[0]]

    out = [jax.ShapeDtypeStruct((1, part, heads * channels), bf16)] * 2
    outs = pl.pallas_call(
        functools.partial(early_kernel, channels, EARLY),
        in_specs=[whole] * (heads + 1),
        out_specs=[anywhere] * 2,
        out_shape=out,
        scratch_shapes=[pltpu.SemaphoreType.DMA((heads + 1, 2))],
        compiler_params=params,
    )(*[arrived[d] for d in EARLY], pieces[0])
    small = (1, states, part)
    grad_in, grad_rate, grad_key, grad_query = pl.pallas_call(
        functools.partial(late_kernel, heads, channels),
        in_specs=[whole] * heads + [anywhere] * 2,
        out_specs=[anywhere] * 4,
        out_shape=out + [jax.ShapeDtypeStruct(small, f32)] * 2,
        scratch_shapes=[pltpu.VMEM(small, f32)] * 2 + [pltpu.SemaphoreType.DMA((heads, 2))],
        input_output_aliases={heads: 0, heads + 1: 1},
        compiler_params=params,
    )(*late, *outs)
    return (grad_in, grad_rate, jnp.swapaxes(grad_key, 1, 2), jnp.swapaxes(grad_query, 1, 2))


def solution(mesh):
    placed = (
        P("dp", "ctx", "head"),
        P("dp", "ctx", "head"),
        P("dp", "ctx", None),
        P("dp", "ctx", None),
        P("dp", "ctx", "head"),
    )
    spread = P("dp", ("ctx", "head"), None)
    return jax.shard_map(
        shards, mesh=mesh, in_specs=placed, out_specs=(spread,) * 4, check_vma=False
    )
```

```python
import functools

import jax
import jax.numpy as jnp
from jax import lax
from jax.experimental import pallas as pl
from jax.experimental.pallas import tpu as pltpu
from jax.sharding import PartitionSpec as P

BLOCK = 16
LANES = 128
SUB = 8
UNROLL = 8
FIRST_TILES = 6
EARLY = (0, 2, 3, 1)
VMEM_LIMIT = 20 * 1024 * 1024


def affine(earlier, subsequent):
    return (earlier[0] * subsequent[0], subsequent[0] * earlier[1] + subsequent[1])


def prefix(array, axis, identity, reverse):
    size, position = (lax.axis_size(axis), lax.axis_index(axis))
    everything = jax.tree.map(lambda part: lax.all_gather(part, axis), array)
    start = jax.tree.map(
        lambda part, zero: jnp.broadcast_to(jnp.asarray(zero, part.dtype), part.shape),
        array,
        identity,
    )

    def hop(k, before):
        at = size - 1 - k if reverse else k
        reached = at > position if reverse else at < position
        new = affine(before, jax.tree.map(lambda part: part[at], everything))
        return jax.tree.map(lambda a, b: jnp.where(reached, a, b), new, before)

    return lax.fori_loop(0, size, hop, start)


def group_summary(inputs, step_rate, key_rows, query_rows, grad_out):
    tokens, channels = inputs.shape[1:]
    state_dim = key_rows.shape[2]
    num_blocks = tokens // BLOCK

    def to_blocks(array_in):
        return array_in[0].astype(jnp.float32).reshape(num_blocks, BLOCK, array_in.shape[2])

    def summarize(carried, block_in):
        x, rate, key_blk, query_blk, grad_blk = block_in
        keys_sq = key_blk * key_blk
        step = rate / (1.0 + rate * jnp.sum(keys_sq, axis=1)[:, None])
        decays = 1.0 - step[:, None, :] * keys_sq[:, :, None]
        drives = (step * x)[:, None, :] * key_blk[:, :, None]
        before = jnp.cumprod(decays, axis=0)
        suffix = jnp.cumprod(decays[::-1], axis=0)[::-1]
        after = jnp.concatenate([suffix[1:], jnp.ones_like(decays[:1])], axis=0)
        total = before[-1]
        end = jnp.sum(drives * after, axis=0)
        back = jnp.sum(grad_blk[:, None, :] * query_blk[:, :, None] * before, axis=0)
        return (
            carried[0] * total,
            total * carried[1] + end,
            carried[2] + carried[0] * back,
        ), None

    zero = jnp.zeros((state_dim, channels), jnp.float32)
    blocked = tuple(map(to_blocks, (inputs, step_rate, key_rows, query_rows, grad_out)))
    return lax.scan(summarize, (jnp.ones_like(zero), zero, zero), blocked)[0]


def spread_columns(matrix, table_ref):
    rows, tokens = matrix.shape
    for t in range(tokens):
        table_ref[t] = jnp.broadcast_to(matrix[:, t : t + 1], (rows, LANES))


def halves(value):
    return [value[at : at + SUB] for at in range(0, value.shape[0], SUB)]


def row(ref, tile, t):
    return ref[tile, pl.ds(t, SUB, stride=0), :]


def norm_row(ref, t):
    return ref[pl.ds(t, SUB, stride=0), :]


def tile_at(j):
    return pl.ds(j * LANES, LANES)


def lane_sums(values):
    high = values.astype(jnp.bfloat16)
    low = (values - high.astype(jnp.float32)).astype(jnp.bfloat16)
    both = jnp.concatenate([high, low], axis=1)
    ones = jnp.ones((2 * LANES, LANES), jnp.bfloat16)
    return jnp.dot(both, ones, preferred_element_type=jnp.float32)


def first_kernel(offset, width, backwards, has_entry, has_tables, *refs):
    refs = list(refs)
    x_ref, rate_ref, key_ref, query_ref, go_ref = refs[:5]
    del refs[:5]
    entry_ref = refs.pop(0) if has_entry else None
    given = [refs.pop(0), refs.pop(0)] if has_tables else None
    path_ref, end_ref, step_ref, drive_ref, x32_ref, go32_ref, inverse_ref = refs[:7]
    keys_ref, queries_ref = given or refs[7:9]
    states, tokens = key_ref.shape[1:]
    tiles = width // LANES
    fetched = []
    if not has_tables:
        sources = (key_ref, query_ref, rate_ref, x_ref, go_ref)
        kept, semaphores = refs[9:14], refs[14]
        for i, (source, to) in enumerate(zip(sources, kept)):
            if i >= 2:
                source = source.at[:, :, pl.ds(offset, width)]
            fetched.append(pltpu.make_async_copy(source, to, semaphores.at[i]))
            fetched[-1].start()
        key_ref, query_ref, rate_ref, x_ref, go_ref = kept
        fetched[0].wait()
        fetched[1].wait()
    key = key_ref[0].astype(jnp.float32)
    if not has_tables:
        spread_columns(key, keys_ref)
        spread_columns(query_ref[0].astype(jnp.float32), queries_ref)
    key_norm = jnp.sum(key * key, axis=0, keepdims=True)
    norm = jnp.transpose(jnp.broadcast_to(key_norm, (LANES, tokens)))
    for copy in fetched[2:]:
        copy.wait()
    for j in range(tiles):
        at = pl.ds((offset if has_tables else 0) + j * LANES, LANES)
        rate = rate_ref[0, :, at]
        x = x_ref[0, :, at].astype(jnp.float32)
        inverse = 1.0 / (1.0 + rate * norm)
        step = rate * inverse
        inverse_ref[j, :tokens] = inverse
        step_ref[j, :tokens] = step
        x32_ref[j, :tokens] = x
        drive_ref[j, :tokens] = step * x
        go32_ref[j, :tokens] = go_ref[0, :, at].astype(jnp.float32)

    if has_entry:
        entry = [halves(entry_ref[:, tile_at(j)]) for j in range(tiles)]
    else:
        entry = [[jnp.zeros((SUB, LANES), jnp.float32)] * (states // SUB)] * tiles

    def finish(state):
        for j in range(tiles):
            end_ref[:, tile_at(j)] = jnp.concatenate(state[j], axis=0)

    def run_states():
        def block(b, state):
            base = b * UNROLL
            state = [list(part) for part in state]
            for u in range(UNROLL):
                k = halves(keys_ref[base + u])
                k2 = [part * part for part in k]
                for j in range(tiles):
                    step = row(step_ref, j, base + u)
                    drive = row(drive_ref, j, base + u)
                    for h in range(len(k)):
                        state[j][h] = (1.0 - step * k2[h]) * state[j][h] + drive * k[h]
                        path_ref[base + u, pl.ds(h * SUB, SUB), tile_at(j)] = state[j][h]
            return state

        finish(lax.fori_loop(0, tokens // UNROLL, block, entry))

    def run_grads():
        def block(i, state):
            base = tokens - UNROLL - i * UNROLL
            state = [list(part) for part in state]
            for u in reversed(range(UNROLL)):
                k2 = [part * part for part in halves(keys_ref[base + u])]
                q = halves(queries_ref[base + u])
                for j in range(tiles):
                    step = row(step_ref, j, base + u)
                    go = row(go32_ref, j, base + u)
                    for h in range(len(q)):
                        grad = go * q[h] + state[j][h]
                        path_ref[base + u, pl.ds(h * SUB, SUB), tile_at(j)] = grad
                        state[j][h] = (1.0 - step * k2[h]) * grad
            return state

        finish(lax.fori_loop(0, tokens // UNROLL, block, entry))

    choose(backwards, run_grads, run_states)


def choose(flag, if_set, if_not):
    if flag is None:
        group = lax.axis_index("ctx")
        pl.when(group != 0)(if_set)
        pl.when(group == 0)(if_not)
    else:
        (if_set if flag else if_not)()


def second_kernel(onwards_here, last, heads, has_start, *refs):
    refs = list(refs)
    entry_ref, path_ref, step_ref, drive_ref, x32_ref, go32_ref, inverse_ref = refs[:7]
    keys_ref, queries_ref = refs[7:9]
    del refs[:9]
    start_ref = refs.pop(0) if has_start else None
    before = [refs.pop(0) for _ in range(3)] if last else None
    if not last:
        del refs[0]
    piece_refs = refs[:heads]
    key_part_ref, query_part_ref, norm_ref, dot_ref, weighted_ref = refs[heads : heads + 5]
    tokens, states = keys_ref.shape[:2]
    tiles = step_ref.shape[0]
    pair = range(states // SUB)

    def path_at(t, h, j):
        return path_ref[t, pl.ds(h * SUB, SUB), tile_at(j)]

    def step_through(back):
        order = list(reversed(range(UNROLL))) if back else list(range(UNROLL))
        work = [(u, j) for u in order for j in range(tiles)]

        def block(i, state):
            base = tokens - UNROLL - i * UNROLL if back else i * UNROLL
            state = [list(part) for part in state]
            if back:
                top = base + UNROLL - 1
                held = [[path_at(top, h, j) for h in pair] for j in range(tiles)]

            def load(u, j):
                rows = [row(ref, j, base + u) for ref in (step_ref, drive_ref, go32_ref)]
                if not back:
                    return rows, [path_at(base + u, h, j) for h in pair]
                earlier = [path_at(jnp.maximum(base + u - 1, 0), h, j) for h in pair]
                if u == 0:
                    for h in pair:
                        start = start_ref[pl.ds(h * SUB, SUB), tile_at(j)] if has_start else 0.0
                        earlier[h] = jnp.where(base == 0, start, earlier[h])
                return rows, earlier

            ahead = load(*work[0])
            for at, (u, j) in enumerate(work):
                t = base + u
                (step, drive, go), loaded = ahead
                if j == 0:
                    k, q = halves(keys_ref[t]), halves(queries_ref[t])
                    k2 = [part * part for part in k]
                if at + 1 < len(work):
                    ahead = load(*work[at + 1])
                dots, weights, terms = [], [], []
                for h in pair:
                    decay = 1.0 - step * k2[h]
                    if back:
                        grad = go * q[h] + state[j][h]
                        here, previous = held[j][h], loaded[h]
                        held[j][h] = previous
                        state[j][h] = decay * grad
                    else:
                        grad, previous = loaded[h], state[j][h]
                        here = decay * previous + drive * k[h]
                        state[j][h] = here
                    weight = grad * previous
                    dots.append(grad * k[h])
                    weights.append(weight * k2[h])
                    terms += [grad * drive, weight * step, here * go]
                rows = pl.ds(pl.multiple_of(t * SUB, SUB), SUB)
                dot_ref[j, rows, :] = sum(dots[1:], dots[0])
                weighted_ref[j, rows, :] = sum(weights[1:], weights[0])
                sums = terms if j == 0 else [a + b for a, b in zip(sums, terms)]
                if j < tiles - 1:
                    continue
                for h in pair:
                    by_drive, by_decay, by_query = sums[3 * h : 3 * h + 3]
                    rows = pl.ds(pl.multiple_of(t * states + h * SUB, SUB), SUB)
                    by_key = by_drive - (2.0 * k[h]) * by_decay
                    if last:
                        by_key = by_key + before[0][rows, :]
                        by_query = by_query + before[1][rows, :]
                    key_part_ref[rows, :] = by_key
                    query_part_ref[rows, :] = by_query
            return state

        entry = [halves(entry_ref[:, tile_at(j)]) for j in range(tiles)]
        lax.fori_loop(0, tokens // UNROLL, block, entry)

    choose(onwards_here, lambda: step_through(False), lambda: step_through(True))

    part = tokens // heads
    rows = 2 * SUB
    position = lax.axis_index("head")
    width = tiles * LANES
    for d in range(heads):
        for r in range(part // rows):
            base = pl.multiple_of((position ^ d) * part + r * rows, rows)
            norm_sum = before[2][pl.ds(base, rows), :] if last else None
            for j in range(tiles):
                dot, weighted = (
                    sum(ref[j, pl.ds(base * SUB + s, rows, stride=SUB), :] for s in range(SUB))
                    for ref in (dot_ref, weighted_ref)
                )
                step, x, inverse = (
                    ref[j, pl.ds(base, rows), :] for ref in (step_ref, x32_ref, inverse_ref)
                )
                grad_step = x * dot - weighted
                grad_rate = grad_step * inverse * inverse
                to = j * LANES
                piece_refs[d][pl.ds(r * rows, rows), pl.ds(to, LANES)] = (step * dot).astype(
                    jnp.bfloat16
                )
                to += width
                piece_refs[d][pl.ds(r * rows, rows), pl.ds(to, LANES)] = grad_rate.astype(
                    jnp.bfloat16
                )
                term = grad_step * step * step
                norm_sum = term if norm_sum is None else norm_sum + term
            norm_ref[pl.ds(base, rows), :] = norm_sum
    if not last:
        return

    tails_ref = refs[heads + 5]
    lane = lax.broadcasted_iota(jnp.int32, (SUB, LANES), 1)
    for h in range(heads):
        packed = jnp.zeros((SUB, LANES), jnp.float32)
        for i, ref in enumerate((key_part_ref, query_part_ref)):
            here = range(h * part, (h + 1) * part)
            values = ref[pl.ds(h * part * states, part * states), :]
            if i == 0:
                norms = [
                    2.0 * keys_ref[t] * jnp.concatenate([norm_row(norm_ref, t)] * len(pair), axis=0)
                    for t in here
                ]
                values = values - jnp.concatenate(norms, axis=0)
            sums = lane_sums(values)
            for t in range(part):
                for half in pair:
                    at = t * states + half * SUB
                    to = (i * len(pair) + half) * part + t
                    packed = jnp.where(lane == to, sums[at : at + SUB], packed)
        tails_ref[h] = packed
    for d in range(heads):
        packed = tails_ref[position ^ d]
        high = packed.astype(jnp.bfloat16).astype(jnp.float32)
        both = jnp.concatenate([high, packed - high], axis=0).astype(jnp.bfloat16)
        tail = pl.ds(2 * width, LANES)
        piece_refs[d][:rows, tail] = both
        piece_refs[d][rows:, tail] = jnp.zeros((part - rows, LANES), jnp.bfloat16)


def place(out_refs, piece, d, offset, width, channels, semaphores):
    at = pl.multiple_of((lax.axis_index("head") ^ d) * channels + offset, LANES)
    copies = []
    for i, out in enumerate(out_refs):
        copies.append(
            pltpu.make_async_copy(
                piece.at[:, pl.ds(i * width, width)],
                out.at[0, :, pl.ds(at, width)],
                semaphores.at[i],
            )
        )
        copies[-1].start()
    return copies


def early_kernel(channels, distances, *refs):
    *pieces, own, in_ref, rate_ref, semaphores = refs
    out_refs = (in_ref, rate_ref)
    first = pieces[0].shape[1] // 2
    width = channels - first
    copies = place(out_refs, own, 0, first, width, channels, semaphores.at[len(pieces)])
    for i, d in enumerate(distances):
        copies += place(out_refs, pieces[i], d, 0, first, channels, semaphores.at[i])
    for copy in copies:
        copy.wait()


def late_kernel(heads, channels, *refs):
    pieces = refs[:heads][::-1]
    *out_refs, key_ref, query_ref, key_kept, query_kept, semaphores = refs[heads + 2 :]
    states, part = key_ref.shape[1:]
    width = (pieces[0].shape[1] - LANES) // 2
    copies = []
    for d in range(1, heads):
        copies += place(
            out_refs, pieces[d], d, channels - width, width, channels, semaphores.at[d]
        )
    total = None
    for d in range(heads):
        tail = pl.ds(2 * width, LANES)
        both = pieces[d][: 2 * SUB, tail].astype(jnp.float32)
        both = both[:SUB] + both[SUB:]
        total = both if total is None else total + both
    for i in range(states // SUB):
        key_kept[0, SUB * i : SUB * i + SUB] = total[:, i * part : (i + 1) * part]
        at = states // SUB + i
        query_kept[0, SUB * i : SUB * i + SUB] = total[:, at * part : (at + 1) * part]
    for i, (kept, out) in enumerate(((key_kept, key_ref), (query_kept, query_ref))):
        copies.append(pltpu.make_async_copy(kept, out, semaphores.at[0, i]))
        copies[-1].start()
    for copy in copies:
        copy.wait()


def shards(inputs, step_rate, key_rows, query_rows, grad_out):
    _, tokens, channels = inputs.shape
    states = key_rows.shape[2]
    heads = lax.axis_size("head")
    groups = lax.axis_size("ctx")
    part = tokens // heads
    tiles = channels // LANES
    first_width = tiles * FIRST_TILES // 8 * LANES
    widths = (first_width, channels - first_width)
    key_cols = jnp.swapaxes(key_rows, 1, 2)
    query_cols = jnp.swapaxes(query_rows, 1, 2)
    f32 = jnp.float32
    bf16 = jnp.bfloat16
    params = pltpu.CompilerParams(vmem_limit_bytes=VMEM_LIMIT)
    whole = pl.BlockSpec(memory_space=pltpu.VMEM)
    anywhere = pl.BlockSpec(memory_space=pl.ANY)
    table = pltpu.VMEM((tokens, states, LANES), f32)

    def cost(width, passes):
        elements = tokens * states * width
        return pl.CostEstimate(
            flops=passes * elements, bytes_accessed=4 * elements, transcendentals=0
        )

    def first(c, backwards, tables=(), entry=None):
        width = widths[c]
        arrays = [inputs, step_rate, key_cols, query_cols, grad_out]
        specs, scratch = [whole] * 5, []
        if c == 0:
            specs = [anywhere] * 5
            arrays = [pltpu.with_memory_space_constraint(a, pltpu.HBM) for a in arrays]
            scratch = [pltpu.VMEM((1, states, tokens), bf16)] * 2
            scratch += [pltpu.VMEM((1, tokens, width), a.dtype) for a in (step_rate, inputs, grad_out)]
            scratch += [pltpu.SemaphoreType.DMA((5,))]
        extra = [*(() if entry is None else (entry,)), *tables[:2]]
        out_shape = [
            pltpu.VMEM((tokens, states, width), f32),
            jax.ShapeDtypeStruct((states, width), f32),
        ]
        out_shape += [pltpu.VMEM((width // LANES, tokens + SUB, LANES), f32)] * 5
        if not tables:
            out_shape += [table] * 2
        path, end, *carried = pl.pallas_call(
            functools.partial(
                first_kernel, sum(widths[:c]), width, backwards, entry is not None, bool(tables)
            ),
            in_specs=specs + [whole] * len(extra),
            out_specs=[whole] * len(out_shape),
            out_shape=out_shape,
            scratch_shapes=scratch,
            compiler_params=params,
            cost_estimate=cost(width, 5),
        )(*arrays, *extra)
        return path, end, carried[:5], tuple(tables) or tuple(carried[5:])

    def second(c, onwards_here, entry, carried, tables, start, before):
        width = widths[c]
        last = c == 1
        keys, queries = tables
        extra = [*(() if start is None else (start,)), *before]
        specs = [whole] * (9 + len(extra))
        if not last:
            extra, specs = extra + [work[1][1][0]], specs + [anywhere]
        parts = pltpu.VMEM((width // LANES, (tokens + 1) * SUB, LANES), f32)
        sums = pltpu.VMEM(((tokens + 1) * states, LANES), f32)
        pieces = [jax.ShapeDtypeStruct((part, 2 * width + LANES * last), bf16)] * heads
        results = pl.pallas_call(
            functools.partial(second_kernel, onwards_here, last, heads, start is not None),
            in_specs=specs,
            out_specs=[whole] * (heads + 3),
            out_shape=pieces + [sums, sums, pltpu.VMEM((tokens + SUB, LANES), f32)],
            scratch_shapes=[parts, parts] + [pltpu.VMEM((heads, SUB, LANES), f32)] * last,
            compiler_params=params,
            cost_estimate=cost(width, 20),
        )(entry, *carried, keys, queries, *extra)
        return results[:heads], results[heads:]

    entries = starts = here = None
    if groups != 2:
        here = False
        product, end, back = group_summary(inputs, step_rate, key_rows, query_rows, grad_out)
        unit = (jnp.ones_like(product), jnp.zeros_like(product))
        starts = prefix((product, end), "ctx", unit, False)[1]
        entries = prefix((product, back), "ctx", unit, True)[1]

    def part_of(array, c):
        return None if array is None else array[:, sum(widths[:c]) : sum(widths[: c + 1])]

    def send(piece, d):
        return lax.ppermute(piece, "head", [(s, s ^ d) for s in range(heads)])

    tables, work = (), []
    for c in range(2):
        path, end, carried, tables = first(c, here, tables, part_of(starts, c))
        entry = part_of(entries, c)
        if entry is None:
            entry = lax.ppermute(end, "ctx", [(0, 1), (1, 0)])
        work.append((entry, [path, *carried], part_of(starts, c)))

    def call_second(c, before):
        entry, carried, start = work[c]
        return second(c, here, entry, carried, tables, start, before)

    away = list(range(heads - 1, 0, -1))
    pieces, before = call_second(0, ())
    arrived = {d: send(pieces[d], d) for d in away}
    arrived[0] = pieces[0]
    pieces, _ = call_second(1, before)
    late = [*(send(pieces[d], d) for d in away), pieces[0]]

    out = [jax.ShapeDtypeStruct((1, part, heads * channels), bf16)] * 2
    outs = pl.pallas_call(
        functools.partial(early_kernel, channels, EARLY),
        in_specs=[whole] * (heads + 1),
        out_specs=[anywhere] * 2,
        out_shape=out,
        scratch_shapes=[pltpu.SemaphoreType.DMA((heads + 1, 2))],
        compiler_params=params,
    )(*[arrived[d] for d in EARLY], pieces[0])
    small = (1, states, part)
    grad_in, grad_rate, grad_key, grad_query = pl.pallas_call(
        functools.partial(late_kernel, heads, channels),
        in_specs=[whole] * heads + [anywhere] * 2,
        out_specs=[anywhere] * 4,
        out_shape=out + [jax.ShapeDtypeStruct(small, f32)] * 2,
        scratch_shapes=[pltpu.VMEM(small, f32)] * 2 + [pltpu.SemaphoreType.DMA((heads, 2))],
        input_output_aliases={heads: 0, heads + 1: 1},
        compiler_params=params,
    )(*late, *outs)
    return (grad_in, grad_rate, jnp.swapaxes(grad_key, 1, 2), jnp.swapaxes(grad_query, 1, 2))


def solution(mesh):
    placed = (
        P("dp", "ctx", "head"),
        P("dp", "ctx", "head"),
        P("dp", "ctx", None),
        P("dp", "ctx", None),
        P("dp", "ctx", "head"),
    )
    spread = P("dp", ("ctx", "head"), None)
    return jax.shard_map(
        shards, mesh=mesh, in_specs=placed, out_specs=(spread,) * 4, check_vma=False
    )
```
